32 devices in a mesh: groups: 2 (over y), curve: 4 (over z), sub: 2 (over x), pair: 2 (over core).
Axes of the slice: x: 2, y: 2, z: 4, core: 2. Of those that a mesh axis runs over, the one named last changes fastest.
Arguments:
- old_dynamics: float32 [10, 128, 4096], P('groups', 'curve', ('sub', 'pair')), parts along dimension 0, may hold values from -6 to 6
- old_area: float32 [10, 128, 4096], P('groups', 'curve', ('sub', 'pair')), parts along dimension 0, may hold values from 0.02 to 0.19
- old_volume: float32 [10, 128, 4096], P('groups', 'curve', ('sub', 'pair')), parts along dimension 0, may hold values from 0.05 to 1
- old_block: int32 [128], replicated, may hold values from 0 to 127, as said below
- wind_stress: float32 [2, 1024, 1024], P(None, ('groups', 'curve'), ('sub', 'pair')), parts along dimension 1, may hold values from -6 to 6
- ice_mask: int32 [1024, 1024], P(('groups', 'curve'), ('sub', 'pair')), parts along dimension 0, may hold values 0 or 1
Outputs:
- velocity: float32 [2, 1024, 1024], P(None, ('groups', 'curve'), ('sub', 'pair')), parts along dimension 1
- stress: float32 [3, 1024, 1024], P(None, ('groups', 'curve'), ('sub', 'pair')), parts along dimension 1
The draws below stay inside these ranges and needn't reach their ends.
There are 2 independent parts, one for each index of `groups`. The reference program is written for one: setup_inputs(seed, part) draws one part's arguments, and reference() takes and returns one part's arrays. A program takes and returns all parts, laid end to end along the dimension named above; an argument that names none is the same for every part. Nothing has to cross between parts.
Inputs may be any that keep to these rules, and one draw needn't show every extreme that they name: `old_block`: A permutation: entry i names the block in old slot i, which lies on curve owner i // 32; block b belongs to new owner b // 32 and has the same slot number b % (32) in both layouts. Each owner sends exactly 2 blocks to each of 3 other owners and keeps the rest.
All inputs are finite; a program needn't handle non-finite values. No bound on the sum of `ice_mask` on one device may be relied on, other than what follows from the above.
Results may differ from the reference program's by a relative error of at most 0.00002.
Values sent between devices are 32-bit elements; how exact they have to be, the bound alone decides.
A program may use at most 64 MiB of HBM per device.

```python
import math
import jax
import jax.numpy as jnp
from jax import lax

BS = 32
RB = 4
CB = 8
NCAT = 5
SUB = 6
MOST = 2
SHIFTS = 3
SLOTS = 128
CELLS = 4096
NY = 512
NX = 1024
N_CURVE = 4
N_SUB = 2
N_PAIR = 2


def draw_old_block(key, part):
    key = jax.random.fold_in(key, 11)
    key_label, key_shift, key_order = jax.random.split(key, 3)
    slot_count = RB * CB
    owners = SLOTS // slot_count
    relabel = jax.random.permutation(key_label, owners).astype(jnp.int32)
    position = jnp.argsort(relabel).astype(jnp.int32)
    offsets = (jax.random.permutation(key_shift, owners - 1)[:SHIFTS] + 1).astype(jnp.int32)
    per_slot = jnp.concatenate([jnp.repeat(offsets, MOST), jnp.zeros((slot_count - MOST * SHIFTS,), jnp.int32)])
    per_slot = per_slot[jax.random.permutation(key_order, slot_count)]
    owner_ids = jnp.arange(owners, dtype=jnp.int32)[:, None]
    slot_ids = jnp.arange(slot_count, dtype=jnp.int32)[None, :]
    target = relabel[(position[owner_ids] + per_slot[slot_ids]) % owners]
    return (target * slot_count + slot_ids).reshape(-1).astype(jnp.int32)


def set_ends(drawn, key, low, top_value):
    spot = [jax.random.randint(jax.random.fold_in(key, axis), (), 0, length) for axis, length in enumerate(drawn.shape)]
    longest = drawn.shape.index(max(drawn.shape))
    beside = spot[:longest] + [(spot[longest] + 1) % drawn.shape[longest]] + spot[longest + 1:]
    return drawn.at[tuple(spot)].set(low).at[tuple(beside)].set(top_value)


def shard_levels(key, dims, cuts, least, high):
    factor_of = 1.0
    for dim, blocks in cuts:
        draws = jax.random.uniform(jax.random.fold_in(jax.random.fold_in(key, 6), dim), (blocks,), jnp.float32, least / len(cuts), high / len(cuts))
        factor_of = factor_of * jnp.repeat(jnp.exp(draws), dims[dim] // blocks).reshape((-1,) + (1,) * (len(dims) - 1 - dim))
    return factor_of


def bell_draw(key, dims, width, bound, shards=(), kind=jnp.bfloat16):
    result = jax.random.normal(key, dims, jnp.float32) * width
    if len(shards) > 0:
        result = shard_levels(key, dims, shards, -0.22, 0.18) * result
    return jnp.clip(result, min=-bound, max=bound).astype(kind)


def setup_inputs(seed: int = 0, part: int = 0) -> dict:
    keys = jax.random.split(jax.random.key(seed), 7)
    part_splits = jax.random.split(jax.random.fold_in(keys[6], part), 7)
    old_dynamics = bell_draw(part_splits[0], (5, SLOTS, CELLS), 1.0, 6.0, ((1, 4), (2, 4)), jnp.float32)
    old_area = jnp.clip(0.02 + 0.17 * jax.random.uniform(part_splits[1], (NCAT, SLOTS, CELLS), jnp.float32) ** shard_levels(part_splits[1], (NCAT, SLOTS, CELLS), ((1, 4), (2, 4)), -0.2, 0.2), 0.02, 0.19)
    old_volume = jnp.clip(jnp.exp(math.log(1.0) - 2.9957323 * jax.random.uniform(part_splits[2], (NCAT, SLOTS, CELLS), jnp.float32) ** shard_levels(part_splits[2], (NCAT, SLOTS, CELLS), ((1, 4), (2, 4)), -0.2, 0.2)), 0.05, 1.0)
    old_block = draw_old_block(jax.random.fold_in(keys[6], 71), part)
    wind_stress = bell_draw(part_splits[4], (2, NY, NX), 1.0, 6.0, ((1, 4), (2, 4)), jnp.float32)
    ice_mask = set_ends((jax.random.randint(part_splits[5], (NY, NX), 0, 4) < 3).astype(jnp.int32), jax.random.fold_in(part_splits[5], 1), 0, 1)
    return dict(old_dynamics=old_dynamics, old_area=old_area, old_volume=old_volume, old_block=old_block, wind_stress=wind_stress, ice_mask=ice_mask)


def derive(area, volume):
    total_area = lax.optimization_barrier(jnp.sum(area, axis=0))
    total_volume = lax.optimization_barrier(jnp.sum(volume, axis=0))
    strength = 2.0 * total_volume * jnp.exp(-2.0 * (1.0 - total_area))
    return jnp.stack([strength, total_volume])

def new_stress(velocity_pad, stress, strength, active):
    along_x = velocity_pad[0]
    along_y = velocity_pad[1]
    du_dx = 0.5 * (along_x[1:-1, 2:] - along_x[1:-1, :-2])
    du_dy = 0.5 * (along_x[2:, 1:-1] - along_x[:-2, 1:-1])
    dv_dx = 0.5 * (along_y[1:-1, 2:] - along_y[1:-1, :-2])
    dv_dy = 0.5 * (along_y[2:, 1:-1] - along_y[:-2, 1:-1])
    divergence = du_dx + dv_dy
    tension = du_dx - dv_dy
    shearing = du_dy + dv_dx
    deformation = jnp.sqrt(divergence * divergence + 0.25 * (tension * tension + shearing * shearing) + 0.25)
    pressure = strength / deformation
    first = active * (stress[0] + 0.5 * pressure * (divergence - deformation)) / 1.5
    second = active * (stress[1] + 0.125 * pressure * tension) / 1.5
    third = active * (stress[2] + 0.0625 * pressure * shearing) / 1.5
    return jnp.stack([first, second, third])

def new_velocity(stress_pad, velocity, ice_mass, wind_stress, active):
    stress_xx = 0.5 * (stress_pad[0] + stress_pad[1])
    stress_yy = 0.5 * (stress_pad[0] - stress_pad[1])
    stress_xy = stress_pad[2]
    force_x = 0.5 * (stress_xx[1:-1, 2:] - stress_xx[1:-1, :-2]) + 0.5 * (stress_xy[2:, 1:-1] - stress_xy[:-2, 1:-1])
    force_y = 0.5 * (stress_xy[1:-1, 2:] - stress_xy[1:-1, :-2]) + 0.5 * (stress_yy[2:, 1:-1] - stress_yy[:-2, 1:-1])
    drag = ice_mass + 0.5
    turning = 0.5 * ice_mass
    determinant = drag * drag + turning * turning
    rhs_x = ice_mass * velocity[0] + force_x + wind_stress[0]
    rhs_y = ice_mass * velocity[1] + force_y + wind_stress[1]
    return jnp.stack([active * (drag * rhs_x + turning * rhs_y) / determinant, active * (drag * rhs_y - turning * rhs_x) / determinant])

def to_grid(blocks):
    field_count = blocks.shape[0]
    shaped = blocks.reshape(field_count, N_CURVE, RB, CB, N_SUB * N_PAIR, BS, BS)
    return shaped.transpose(0, 1, 2, 5, 4, 3, 6).reshape(field_count, NY, NX)

def with_border(field):
    return jnp.pad(field, ((0, 0), (1, 1), (1, 1)))

def reference(old_dynamics, old_area, old_volume, old_block, wind_stress, ice_mask):

    def settle(old):
        return jnp.zeros_like(old).at[:, old_block, :].set(old)
    dynamics = to_grid(settle(old_dynamics))
    derived = derive(to_grid(settle(old_area)), to_grid(settle(old_volume)))
    strength = derived[0]
    ice_mass = derived[1]
    active = ice_mask.astype(jnp.float32)
    velocity = dynamics[0:2]
    stress = dynamics[2:5]
    for subcycle in range(SUB):
        stress = new_stress(with_border(velocity), stress, strength, active)
        velocity = new_velocity(with_border(stress), velocity, ice_mass, wind_stress, active)
    return (velocity, stress)
```

```python
import functools

import jax
import jax.numpy as jnp
from jax import lax
from jax.experimental import pallas as pl
from jax.experimental.pallas import tpu as pltpu
from jax.sharding import PartitionSpec as P

BS = 32
RB = 4
CB = 8
NCAT = 5
SUB = 6
MOST = 2
SLOT = RB * CB
LANES = 128
ROWS = RB * BS
TILES = CB * BS // LANES
CHUNKS = BS * BS // LANES
PER = LANES // BS
WIDE = 2 * SUB
HALO = 16
TOP = 8
CORE = TOP + HALO
LOW = CORE + ROWS
TALL = LOW + HALO + 8
SPAN = ROWS + 2 * HALO
STEP = 32
FIELDS = 7
MESH = pl.DeviceIdType.MESH


def kernel(
    owners, subs, pairs,
    dyn_ref, area_ref, vol_ref, block_ref, wind_ref, mask_ref,
    vel_ref, stress_ref,
    own, area, vol, send, came, grid, mask, edge, side, source,
    in_sem, out_sem, mig_send, mig_recv, halo_send, halo_recv,
):
    me = lax.axis_index("curve")
    col = lax.axis_index("sub") * pairs + lax.axis_index("pair")
    cols = subs * pairs
    has_up, has_down = me > 0, me < owners - 1
    has_left, has_right = col > 0, col < cols - 1

    def device(d_row, d_col):
        there = lax.rem(col + d_col + cols, cols)
        return {
            "curve": lax.rem(me + d_row + owners, owners),
            "sub": lax.div(there, pairs),
            "pair": lax.rem(there, pairs),
        }

    def exists(d_row, d_col):
        flag = None
        for step, low, high in ((d_row, has_up, has_down), (d_col, has_left, has_right)):
            if step:
                part = low if step < 0 else high
                flag = part if flag is None else jnp.logical_and(flag, part)
        return flag

    loads = []
    for t in range(TILES):
        loads.append(pltpu.make_async_copy(
            wind_ref.at[:, :, pl.ds(t * LANES, LANES)],
            grid.at[pl.ds(FIELDS, 2), t, pl.ds(CORE, ROWS), :], in_sem.at[2 * t]))
        loads.append(pltpu.make_async_copy(
            mask_ref.at[:, pl.ds(t * LANES, LANES)], mask.at[t], in_sem.at[2 * t + 1]))
    base = 2 * TILES
    for j in range(CHUNKS):
        lanes = pl.ds(j * LANES, LANES)
        loads.append(pltpu.make_async_copy(area_ref.at[:, :, lanes], area.at[j], in_sem.at[base + 3 * j]))
        loads.append(pltpu.make_async_copy(vol_ref.at[:, :, lanes], vol.at[j], in_sem.at[base + 3 * j + 1]))
        loads.append(pltpu.make_async_copy(
            dyn_ref.at[:, :, lanes], own.at[j, pl.ds(0, 5)], in_sem.at[base + 3 * j + 2]))
    for load in loads:
        load.start()

    rim = jnp.zeros((10, TILES + 1, CORE, LANES), jnp.float32)
    grid[pl.ds(0, 10), :, pl.ds(0, CORE), :] = rim
    grid[pl.ds(0, 10), :, pl.ds(LOW, CORE), :] = rim
    side[...] = jnp.zeros(side.shape, jnp.float32)

    barrier = pltpu.get_barrier_semaphore()

    def greet(k, carry):
        pl.semaphore_signal(barrier, inc=1, device_id={"curve": lax.rem(me + k, owners)}, device_id_type=MESH)
        return carry

    lax.fori_loop(1, owners, greet, 0)
    count = owners - 1
    around = [(0, -1), (0, 1), (-1, -1), (-1, 1), (1, -1), (1, 1)]
    for d_row, d_col in around:
        flag = exists(d_row, d_col)
        count = count + flag.astype(jnp.int32)

        @pl.when(flag)
        def _():
            pl.semaphore_signal(barrier, inc=1, device_id=device(d_row, d_col), device_id_type=MESH)

    pl.semaphore_wait(barrier, count)

    for load in loads[:base]:
        load.wait()
    grid[9, pl.ds(0, TILES), pl.ds(CORE, ROWS), :] = mask[...].astype(jnp.float32)

    def row_copy(d_row, start, length, slot):
        here = CORE if d_row < 0 else LOW - HALO
        there = LOW if d_row < 0 else TOP
        return pltpu.make_async_remote_copy(
            src_ref=grid.at[pl.ds(start, length), pl.ds(0, TILES), pl.ds(here, HALO), :],
            dst_ref=grid.at[pl.ds(start, length), pl.ds(0, TILES), pl.ds(there, HALO), :],
            send_sem=halo_send.at[slot], recv_sem=halo_recv.at[slot],
            device_id=device(d_row, 0), device_id_type=MESH)

    def each(copies, act):
        for flag, copy in copies:
            @pl.when(flag)
            def _():
                act(copy)

    early = [(exists(-1, 0), row_copy(-1, FIELDS, 3, 0)), (exists(1, 0), row_copy(1, FIELDS, 3, 1))]
    early_back = [(exists(1, 0), early[0][1]), (exists(-1, 0), early[1][1])]
    each(early, lambda copy: copy.start())

    for load in loads[base:]:
        load.wait()

    def derive(j, carry):
        total_area = area[j, 0]
        total_volume = vol[j, 0]
        for n in range(1, NCAT):
            total_area = total_area + area[j, n]
            total_volume = total_volume + vol[j, n]
        own[j, 5] = 2.0 * total_volume * jnp.exp(-2.0 * (1.0 - total_area))
        own[j, 6] = total_volume
        return carry

    lax.fori_loop(0, CHUNKS, derive, 0)

    flat = own.reshape(CHUNKS * FIELDS * SLOT, LANES)

    def block_rows(field, slot):
        return flat[pl.ds(field * SLOT + slot, CHUNKS, stride=FIELDS * SLOT), :]

    def migrate(k):
        to = lax.rem(me + k, owners)
        return pltpu.make_async_remote_copy(
            src_ref=send.at[k], dst_ref=came.at[k],
            send_sem=mig_send.at[k], recv_sem=mig_recv.at[k],
            device_id={"curve": to}, device_id_type=MESH)

    def pack(k, carry):
        to = lax.rem(me + k, owners)
        first, last = jnp.int32(SLOT - 1), jnp.int32(0)
        for s in range(SLOT):
            place = block_ref[me * SLOT + s] - to * SLOT
            match = jnp.logical_and(place >= 0, place < SLOT)
            first = jnp.where(match, jnp.minimum(first, s), first)
            last = jnp.where(match, s, last)
        for rank, slot in enumerate((first, last)):
            for f in range(FIELDS):
                send[k, rank, f] = block_rows(f, slot)
        migrate(k).start()
        return carry

    lax.fori_loop(1, owners, pack, 0)

    for p in range(SLOT):
        source[p] = jnp.int32(-1)

    def find(k, carry):
        giver = lax.rem(me + owners - k, owners)
        rank = jnp.int32(0)
        for p in range(SLOT):
            place = block_ref[giver * SLOT + p] - me * SLOT
            match = jnp.logical_and(place >= 0, place < SLOT)
            source[p] = jnp.where(match, k * MOST + jnp.minimum(rank, MOST - 1), source[p])
            rank = jnp.where(match, rank + 1, rank)
        return carry

    lax.fori_loop(1, owners, find, 0)

    def arrive(k, carry):
        migrate(k).wait_recv()
        return carry

    lax.fori_loop(1, owners, arrive, 0)

    lane = lax.broadcasted_iota(jnp.int32, (CHUNKS, LANES), 1)
    upper = lane >= LANES // 2
    odd = lax.rem(lax.div(lane, BS), 2) == 1
    arrivals = came.reshape(owners * MOST, FIELDS, CHUNKS, LANES)

    def settle(r, carry):
        for h in range(TILES):
            slots = []
            for m in range(PER):
                p = r * CB + h * PER + m
                here = source[p]
                slots.append((p, here >= 0, jnp.maximum(here, MOST)))
            for f in range(FIELDS):
                v0, v1, v2, v3 = [
                    jnp.where(new, arrivals[index, f], block_rows(f, p)) for p, new, index in slots
                ]
                a0 = jnp.where(upper, pltpu.roll(v2, 64, 1), v0)
                a2 = jnp.where(upper, v2, pltpu.roll(v0, 64, 1))
                a1 = jnp.where(upper, pltpu.roll(v3, 64, 1), v1)
                a3 = jnp.where(upper, v3, pltpu.roll(v1, 64, 1))
                rows = (
                    jnp.where(odd, pltpu.roll(a1, 32, 1), a0),
                    jnp.where(odd, a1, pltpu.roll(a0, 96, 1)),
                    jnp.where(odd, pltpu.roll(a3, 32, 1), a2),
                    jnp.where(odd, a3, pltpu.roll(a2, 96, 1)),
                )
                for y, value in enumerate(rows):
                    grid[f, h, pl.ds(CORE + r * BS + y, CHUNKS, stride=PER), :] = value
        return carry

    lax.fori_loop(0, RB, settle, 0)

    late = [(exists(-1, 0), row_copy(-1, 0, FIELDS, 2)), (exists(1, 0), row_copy(1, 0, FIELDS, 3))]
    late_back = [(exists(1, 0), late[0][1]), (exists(-1, 0), late[1][1])]
    each(late, lambda copy: copy.start())

    def strips(i, carry):
        start = pl.multiple_of(i * STEP, 8)
        place = lax.broadcasted_iota(jnp.int32, (STEP, LANES), 1)
        left = jnp.zeros((STEP, LANES), jnp.float32)
        right = jnp.zeros((STEP, LANES), jnp.float32)
        for f in range(10):
            inside = jnp.logical_and(place >= f * WIDE, place < (f + 1) * WIDE)
            first = grid[f, 0, pl.ds(CORE + start, STEP), :]
            last = grid[f, TILES - 1, pl.ds(CORE + start, STEP), :]
            if f:
                first = pltpu.roll(first, f * WIDE, 1)
            left = jnp.where(inside, first, left)
            right = jnp.where(inside, pltpu.roll(last, ((f + 1) * WIDE) % LANES, 1), right)
        edge[0, pl.ds(start, STEP), :] = left
        edge[1, pl.ds(start, STEP), :] = right
        return carry

    lax.fori_loop(0, ROWS // STEP, strips, 0)

    def strip_copy(d_row, d_col, slot):
        which = 0 if d_col < 0 else 1
        here, length, there = {
            0: (0, ROWS, HALO), -1: (0, HALO, HALO + ROWS), 1: (ROWS - HALO, HALO, 0),
        }[d_row]
        return pltpu.make_async_remote_copy(
            src_ref=edge.at[which, pl.ds(here, length), :],
            dst_ref=side.at[which, pl.ds(there, length), :],
            send_sem=halo_send.at[slot], recv_sem=halo_recv.at[slot],
            device_id=device(d_row, d_col), device_id_type=MESH)

    columns, columns_back = [], []
    for i, (d_row, d_col) in enumerate(around):
        copy = strip_copy(d_row, d_col, 4 + i)
        columns.append((exists(d_row, d_col), copy))
        columns_back.append((exists(-d_row, -d_col), copy))
    each(columns, lambda copy: copy.start())
    each(early_back + late_back + columns_back, lambda copy: copy.wait_recv())
    each(early + late + columns, lambda copy: copy.wait_send())

    def spread(i, carry):
        start = pl.multiple_of(i * STEP, 8)
        place = lax.broadcasted_iota(jnp.int32, (STEP, LANES), 1)
        from_right = side[0, pl.ds(start, STEP), :]
        from_left = side[1, pl.ds(start, STEP), :]
        for f in range(10):
            first = pltpu.roll(from_right, (LANES - f * WIDE) % LANES, 1) if f else from_right
            last = pltpu.roll(from_left, LANES - (f + 1) * WIDE, 1)
            grid[f, TILES, pl.ds(TOP + start, STEP), :] = jnp.where(
                place < WIDE, first, jnp.where(place >= LANES - WIDE, last, 0.0))
        for t in range(TILES + 1):
            rows = pl.ds(TOP + start, STEP)
            active = grid[9, t, rows, :]
            strength = grid[5, t, rows, :]
            mass = grid[6, t, rows, :]
            drag = mass + 0.5
            turning = 0.5 * mass
            scale = active / (drag * drag + turning * turning)
            keep = active * (1.0 / 1.5)
            grid[9, t, rows, :] = keep
            grid[5, t, rows, :] = 0.5 * keep * strength
            grid[10, t, rows, :] = scale * drag
            grid[11, t, rows, :] = scale * turning
        return carry

    lax.fori_loop(0, SPAN // STEP, spread, 0)

    all_tiles = range(TILES + 1)
    place = lax.broadcasted_iota(jnp.int32, (STEP, LANES), 1)
    is_first, is_last = place == 0, place == LANES - 1

    def across(values):
        ahead = [pltpu.roll(x, LANES - 1, 1) for x in values]
        behind = [pltpu.roll(x, 1, 1) for x in values]
        n = len(values)
        return [
            jnp.where(is_last, ahead[(t + 1) % n], ahead[t]) - jnp.where(is_first, behind[(t - 1) % n], behind[t])
            for t in range(n)
        ]

    def stress_rows(i, carry):
        start = pl.multiple_of(TOP + i * STEP, 8)
        rows = pl.ds(start, STEP)
        above, below = pl.ds(start - 1, STEP), pl.ds(start + 1, STEP)
        u_x = across([grid[0, t, rows, :] for t in all_tiles])
        v_x = across([grid[1, t, rows, :] for t in all_tiles])
        for t in all_tiles:
            u_y = grid[0, t, below, :] - grid[0, t, above, :]
            v_y = grid[1, t, below, :] - grid[1, t, above, :]
            divergence = u_x[t] + v_y
            tension = u_x[t] - v_y
            shearing = u_y + v_x[t]
            inverse = lax.rsqrt(divergence * divergence + 0.25 * (tension * tension + shearing * shearing) + 1.0)
            keep = grid[9, t, rows, :]
            force = grid[5, t, rows, :]
            scaled = force * inverse
            grid[2, t, rows, :] = keep * grid[2, t, rows, :] + (scaled * divergence - force)
            grid[3, t, rows, :] = keep * grid[3, t, rows, :] + 0.25 * (scaled * tension)
            grid[4, t, rows, :] = keep * grid[4, t, rows, :] + 0.125 * (scaled * shearing)
        return carry

    def velocity_rows(i, carry):
        start = pl.multiple_of(TOP + i * STEP, 8)
        rows = pl.ds(start, STEP)
        above, below = pl.ds(start - 1, STEP), pl.ds(start + 1, STEP)
        sum_x = across([grid[2, t, rows, :] + grid[3, t, rows, :] for t in all_tiles])
        cross_x = across([grid[4, t, rows, :] for t in all_tiles])
        for t in all_tiles:
            cross_y = grid[4, t, below, :] - grid[4, t, above, :]
            lower = grid[2, t, below, :] - grid[3, t, below, :]
            higher = grid[2, t, above, :] - grid[3, t, above, :]
            mass = grid[6, t, rows, :]
            rhs_x = mass * grid[0, t, rows, :] + (0.25 * sum_x[t] + 0.5 * cross_y) + grid[7, t, rows, :]
            rhs_y = mass * grid[1, t, rows, :] + (0.5 * cross_x[t] + 0.25 * (lower - higher)) + grid[8, t, rows, :]
            ahead = grid[10, t, rows, :]
            turn = grid[11, t, rows, :]
            grid[0, t, rows, :] = ahead * rhs_x + turn * rhs_y
            grid[1, t, rows, :] = ahead * rhs_y - turn * rhs_x
        return carry

    def subcycle(n, carry):
        lax.fori_loop(0, SPAN // STEP, stress_rows, 0)
        lax.fori_loop(0, SPAN // STEP, velocity_rows, 0)
        return carry

    lax.fori_loop(0, SUB, subcycle, 0)

    stores = []
    for t in range(TILES):
        lanes = pl.ds(t * LANES, LANES)
        stores.append(pltpu.make_async_copy(
            grid.at[pl.ds(0, 2), t, pl.ds(CORE, ROWS), :], vel_ref.at[:, :, lanes], out_sem.at[2 * t]))
        stores.append(pltpu.make_async_copy(
            grid.at[pl.ds(2, 3), t, pl.ds(CORE, ROWS), :], stress_ref.at[:, :, lanes], out_sem.at[2 * t + 1]))
    for store in stores:
        store.start()

    def sent(k, carry):
        migrate(k).wait_send()
        return carry

    lax.fori_loop(1, owners, sent, 0)
    for store in stores:
        store.wait()


def shards(old_dynamics, old_area, old_volume, old_block, wind_stress, ice_mask):
    owners, subs, pairs = (lax.axis_size(name) for name in ("curve", "sub", "pair"))
    anywhere = pl.BlockSpec(memory_space=pl.ANY)
    real = jnp.float32
    return pl.pallas_call(
        functools.partial(kernel, owners, subs, pairs),
        out_shape=(
            jax.ShapeDtypeStruct((2, ROWS, CB * BS), real),
            jax.ShapeDtypeStruct((3, ROWS, CB * BS), real),
        ),
        in_specs=[anywhere] * 3 + [pl.BlockSpec(memory_space=pltpu.SMEM)] + [anywhere] * 2,
        out_specs=(anywhere, anywhere),
        scratch_shapes=[
            pltpu.VMEM((CHUNKS, FIELDS, SLOT, LANES), real),
            pltpu.VMEM((CHUNKS, NCAT, SLOT, LANES), real),
            pltpu.VMEM((CHUNKS, NCAT, SLOT, LANES), real),
            pltpu.VMEM((owners, MOST, FIELDS, CHUNKS, LANES), real),
            pltpu.VMEM((owners, MOST, FIELDS, CHUNKS, LANES), real),
            pltpu.VMEM((12, TILES + 1, TALL, LANES), real),
            pltpu.VMEM((TILES, ROWS, LANES), jnp.int32),
            pltpu.VMEM((2, ROWS, LANES), real),
            pltpu.VMEM((2, SPAN, LANES), real),
            pltpu.SMEM((SLOT,), jnp.int32),
            pltpu.SemaphoreType.DMA((2 * TILES + 3 * CHUNKS,)),
            pltpu.SemaphoreType.DMA((2 * TILES,)),
            pltpu.SemaphoreType.DMA((owners,)),
            pltpu.SemaphoreType.DMA((owners,)),
            pltpu.SemaphoreType.DMA((10,)),
            pltpu.SemaphoreType.DMA((10,)),
        ],
        compiler_params=pltpu.CompilerParams(
            collective_id=0, has_side_effects=True, vmem_limit_bytes=40 * 1024 * 1024
        ),
    )(old_dynamics, old_area, old_volume, old_block, wind_stress, ice_mask)


def solution(mesh):
    return jax.shard_map(
        shards,
        mesh=mesh,
        in_specs=(
            P("groups", "curve", ("sub", "pair")),
            P("groups", "curve", ("sub", "pair")),
            P("groups", "curve", ("sub", "pair")),
            P(),
            P(None, ("groups", "curve"), ("sub", "pair")),
            P(("groups", "curve"), ("sub", "pair")),
        ),
        out_specs=(
            P(None, ("groups", "curve"), ("sub", "pair")),
            P(None, ("groups", "curve"), ("sub", "pair")),
        ),
        check_vma=False,
    )
```

```python
import functools

import jax
import jax.numpy as jnp
from jax import lax
from jax.experimental import pallas as pl
from jax.experimental.pallas import tpu as pltpu
from jax.sharding import PartitionSpec as P

BS = 32
RB = 4
CB = 8
NCAT = 5
SUB = 6
MOST = 2
SLOT = RB * CB
LANES = 128
ROWS = RB * BS
TILES = CB * BS // LANES
CHUNKS = BS * BS // LANES
PER = LANES // BS
WIDE = 2 * SUB
HALO = 16
TOP = 8
CORE = TOP + HALO
LOW = CORE + ROWS
TALL = LOW + HALO + 8
SPAN = ROWS + 2 * HALO
STEP = 32
PIECE = 16
UNROLL = True
LIMIT = 56
FIELDS = 7
MESH = pl.DeviceIdType.MESH


def kernel(
    owners, subs, pairs,
    dyn_ref, area_ref, vol_ref, block_ref, wind_ref, mask_ref,
    vel_out, stress_out,
    vel_ref, stress_ref, fixed_ref, final, own, area, vol, send, came, grid, mask, edge, side, source,
    in_sem, out_sem, mig_send, mig_recv, halo_send, halo_recv,
):
    me = lax.axis_index("curve")
    col = lax.axis_index("sub") * pairs + lax.axis_index("pair")
    cols = subs * pairs
    has_up, has_down = me > 0, me < owners - 1
    has_left, has_right = col > 0, col < cols - 1

    def device(d_row, d_col):
        there = lax.rem(col + d_col + cols, cols)
        return {
            "curve": lax.rem(me + d_row + owners, owners),
            "sub": lax.div(there, pairs),
            "pair": lax.rem(there, pairs),
        }

    def exists(d_row, d_col):
        flag = None
        for step, low, high in ((d_row, has_up, has_down), (d_col, has_left, has_right)):
            if step:
                part = low if step < 0 else high
                flag = part if flag is None else jnp.logical_and(flag, part)
        return flag

    loads = []
    for t in range(TILES):
        loads.append(pltpu.make_async_copy(
            wind_ref.at[:, :, pl.ds(t * LANES, LANES)],
            grid.at[pl.ds(FIELDS, 2), t, pl.ds(CORE, ROWS), :], in_sem.at[2 * t]))
        loads.append(pltpu.make_async_copy(
            mask_ref.at[:, pl.ds(t * LANES, LANES)], mask.at[t], in_sem.at[2 * t + 1]))
    base = 2 * TILES
    for j in range(CHUNKS):
        lanes = pl.ds(j * LANES, LANES)
        loads.append(pltpu.make_async_copy(area_ref.at[:, :, lanes], area.at[j], in_sem.at[base + 3 * j]))
        loads.append(pltpu.make_async_copy(vol_ref.at[:, :, lanes], vol.at[j], in_sem.at[base + 3 * j + 1]))
        loads.append(pltpu.make_async_copy(
            dyn_ref.at[:, :, lanes], own.at[j, pl.ds(0, 5)], in_sem.at[base + 3 * j + 2]))
    for load in loads:
        load.start()

    rim = jnp.zeros((10, TILES, CORE, LANES), jnp.float32)
    grid[:, :, pl.ds(0, CORE), :] = rim
    grid[:, :, pl.ds(LOW, CORE), :] = rim
    for ref in (vel_ref, stress_ref):
        pad = jnp.zeros((ref.shape[0], TILES + 1, TOP, LANES), jnp.float32)
        ref[:, :, pl.ds(0, TOP), :] = pad
        ref[:, :, pl.ds(TALL - TOP, TOP), :] = pad
    side[...] = jnp.zeros(side.shape, jnp.float32)

    barrier = pltpu.get_barrier_semaphore()

    def greet(k, carry):
        pl.semaphore_signal(barrier, inc=1, device_id={"curve": lax.rem(me + k, owners)}, device_id_type=MESH)
        return carry

    lax.fori_loop(1, owners, greet, 0)
    count = owners - 1
    around = [(0, -1), (0, 1), (-1, -1), (-1, 1), (1, -1), (1, 1)]
    for d_row, d_col in around:
        flag = exists(d_row, d_col)
        count = count + flag.astype(jnp.int32)

        @pl.when(flag)
        def _():
            pl.semaphore_signal(barrier, inc=1, device_id=device(d_row, d_col), device_id_type=MESH)

    pl.semaphore_wait(barrier, count)

    for load in loads[:base]:
        load.wait()
    grid[9, pl.ds(0, TILES), pl.ds(CORE, ROWS), :] = mask[...].astype(jnp.float32)

    def row_copy(d_row, start, length, slot):
        here = CORE if d_row < 0 else LOW - HALO
        there = LOW if d_row < 0 else TOP
        return pltpu.make_async_remote_copy(
            src_ref=grid.at[pl.ds(start, length), pl.ds(0, TILES), pl.ds(here, HALO), :],
            dst_ref=grid.at[pl.ds(start, length), pl.ds(0, TILES), pl.ds(there, HALO), :],
            send_sem=halo_send.at[slot], recv_sem=halo_recv.at[slot],
            device_id=device(d_row, 0), device_id_type=MESH)

    def each(copies, act):
        for flag, copy in copies:
            @pl.when(flag)
            def _():
                act(copy)

    early = [(exists(-1, 0), row_copy(-1, FIELDS, 3, 0)), (exists(1, 0), row_copy(1, FIELDS, 3, 1))]
    early_back = [(exists(1, 0), early[0][1]), (exists(-1, 0), early[1][1])]
    each(early, lambda copy: copy.start())

    for load in loads[base:]:
        load.wait()

    def derive(j, carry):
        total_area = area[j, 0]
        total_volume = vol[j, 0]
        for n in range(1, NCAT):
            total_area = total_area + area[j, n]
            total_volume = total_volume + vol[j, n]
        own[j, 5] = 2.0 * total_volume * jnp.exp(-2.0 * (1.0 - total_area))
        own[j, 6] = total_volume
        return carry

    lax.fori_loop(0, CHUNKS, derive, 0)

    flat = own.reshape(CHUNKS * FIELDS * SLOT, LANES)

    def block_rows(field, slot):
        return flat[pl.ds(field * SLOT + slot, CHUNKS, stride=FIELDS * SLOT), :]

    def migrate(k):
        to = lax.rem(me + k, owners)
        return pltpu.make_async_remote_copy(
            src_ref=send.at[k], dst_ref=came.at[k],
            send_sem=mig_send.at[k], recv_sem=mig_recv.at[k],
            device_id={"curve": to}, device_id_type=MESH)

    def pack(k, carry):
        to = lax.rem(me + k, owners)
        first, last = jnp.int32(SLOT - 1), jnp.int32(0)
        for s in range(SLOT):
            place = block_ref[me * SLOT + s] - to * SLOT
            match = jnp.logical_and(place >= 0, place < SLOT)
            first = jnp.where(match, jnp.minimum(first, s), first)
            last = jnp.where(match, s, last)
        for rank, slot in enumerate((first, last)):
            for f in range(FIELDS):
                send[k, rank, f] = block_rows(f, slot)
        migrate(k).start()
        return carry

    lax.fori_loop(1, owners, pack, 0)

    for p in range(SLOT):
        source[p] = jnp.int32(-1)

    def find(k, carry):
        giver = lax.rem(me + owners - k, owners)
        rank = jnp.int32(0)
        for p in range(SLOT):
            place = block_ref[giver * SLOT + p] - me * SLOT
            match = jnp.logical_and(place >= 0, place < SLOT)
            source[p] = jnp.where(match, k * MOST + jnp.minimum(rank, MOST - 1), source[p])
            rank = jnp.where(match, rank + 1, rank)
        return carry

    lax.fori_loop(1, owners, find, 0)

    def arrive(k, carry):
        migrate(k).wait_recv()
        return carry

    lax.fori_loop(1, owners, arrive, 0)

    lane = lax.broadcasted_iota(jnp.int32, (CHUNKS, LANES), 1)
    upper = lane >= LANES // 2
    odd = lax.rem(lax.div(lane, BS), 2) == 1
    arrivals = came.reshape(owners * MOST, FIELDS, CHUNKS, LANES)

    def settle(r, carry):
        for h in range(TILES):
            slots = []
            for m in range(PER):
                p = r * CB + h * PER + m
                here = source[p]
                slots.append((p, here >= 0, jnp.maximum(here, MOST)))
            for f in range(FIELDS):
                v0, v1, v2, v3 = [
                    jnp.where(new, arrivals[index, f], block_rows(f, p)) for p, new, index in slots
                ]
                a0 = jnp.where(upper, pltpu.roll(v2, 64, 1), v0)
                a2 = jnp.where(upper, v2, pltpu.roll(v0, 64, 1))
                a1 = jnp.where(upper, pltpu.roll(v3, 64, 1), v1)
                a3 = jnp.where(upper, v3, pltpu.roll(v1, 64, 1))
                rows = (
                    jnp.where(odd, pltpu.roll(a1, 32, 1), a0),
                    jnp.where(odd, a1, pltpu.roll(a0, 96, 1)),
                    jnp.where(odd, pltpu.roll(a3, 32, 1), a2),
                    jnp.where(odd, a3, pltpu.roll(a2, 96, 1)),
                )
                for y, value in enumerate(rows):
                    grid[f, h, pl.ds(CORE + r * BS + y, CHUNKS, stride=PER), :] = value
        return carry

    lax.fori_loop(0, RB, settle, 0)

    late = [(exists(-1, 0), row_copy(-1, 0, FIELDS, 2)), (exists(1, 0), row_copy(1, 0, FIELDS, 3))]
    late_back = [(exists(1, 0), late[0][1]), (exists(-1, 0), late[1][1])]
    each(late, lambda copy: copy.start())

    def strips(i, carry):
        start = pl.multiple_of(i * STEP, 8)
        place = lax.broadcasted_iota(jnp.int32, (STEP, LANES), 1)
        left = jnp.zeros((STEP, LANES), jnp.float32)
        right = jnp.zeros((STEP, LANES), jnp.float32)
        for f in range(10):
            inside = jnp.logical_and(place >= f * WIDE, place < (f + 1) * WIDE)
            first = grid[f, 0, pl.ds(CORE + start, STEP), :]
            last = grid[f, TILES - 1, pl.ds(CORE + start, STEP), :]
            if f:
                first = pltpu.roll(first, f * WIDE, 1)
            left = jnp.where(inside, first, left)
            right = jnp.where(inside, pltpu.roll(last, ((f + 1) * WIDE) % LANES, 1), right)
        edge[0, pl.ds(start, STEP), :] = left
        edge[1, pl.ds(start, STEP), :] = right
        return carry

    lax.fori_loop(0, ROWS // STEP, strips, 0)

    def strip_copy(d_row, d_col, slot):
        which = 0 if d_col < 0 else 1
        here, length, there = {
            0: (0, ROWS, HALO), -1: (0, HALO, HALO + ROWS), 1: (ROWS - HALO, HALO, 0),
        }[d_row]
        return pltpu.make_async_remote_copy(
            src_ref=edge.at[which, pl.ds(here, length), :],
            dst_ref=side.at[which, pl.ds(there, length), :],
            send_sem=halo_send.at[slot], recv_sem=halo_recv.at[slot],
            device_id=device(d_row, d_col), device_id_type=MESH)

    columns, columns_back = [], []
    for i, (d_row, d_col) in enumerate(around):
        copy = strip_copy(d_row, d_col, 4 + i)
        columns.append((exists(d_row, d_col), copy))
        columns_back.append((exists(-d_row, -d_col), copy))
    each(columns, lambda copy: copy.start())
    each(early_back + late_back + columns_back, lambda copy: copy.wait_recv())

    def spread(i, carry):
        start = pl.multiple_of(i * STEP, 8)
        place = lax.broadcasted_iota(jnp.int32, (STEP, LANES), 1)
        from_right = side[0, pl.ds(start, STEP), :]
        from_left = side[1, pl.ds(start, STEP), :]
        rows = pl.ds(TOP + start, STEP)
        values = []
        for f in range(10):
            first = pltpu.roll(from_right, (LANES - f * WIDE) % LANES, 1) if f else from_right
            last = pltpu.roll(from_left, LANES - (f + 1) * WIDE, 1)
            beyond = jnp.where(place < WIDE, first, jnp.where(place >= LANES - WIDE, last, 0.0))
            values.append([grid[f, t, rows, :] for t in range(TILES)] + [beyond])
        for t in range(TILES + 1):
            u, v, s1, s2, s12, strength, mass, wind_x, wind_y, active = [value[t] for value in values]
            drag = mass + 0.5
            turning = 0.5 * mass
            scale = active / (drag * drag + turning * turning)
            keep = active * (1.0 / 1.5)
            vel_ref[0, t, rows, :] = u
            vel_ref[1, t, rows, :] = v
            stress_ref[0, t, rows, :] = 0.25 * s1
            stress_ref[1, t, rows, :] = 0.25 * s2
            stress_ref[2, t, rows, :] = 0.5 * s12
            fixed_ref[0, t, rows, :] = keep
            fixed_ref[1, t, rows, :] = 0.125 * keep * strength
            fixed_ref[2, t, rows, :] = mass
            fixed_ref[3, t, rows, :] = wind_x
            fixed_ref[4, t, rows, :] = wind_y
            fixed_ref[5, t, rows, :] = scale * drag
            fixed_ref[6, t, rows, :] = scale * turning
        return carry

    lax.fori_loop(0, SPAN // STEP, spread, 0)

    cycles(vel_out, stress_out, vel_ref, stress_ref, fixed_ref, final, out_sem)

    def sent(k, carry):
        migrate(k).wait_send()
        return carry

    lax.fori_loop(1, owners, sent, 0)
    each(early + late + columns, lambda copy: copy.wait_send())


def cycles(vel_out, stress_out, vel, stress, fixed, final, out_sem):
    tiles = range(TILES + 1)
    place = lax.broadcasted_iota(jnp.int32, (PIECE, LANES), 1)
    is_first, is_last = place == 0, place == LANES - 1

    def across(values):
        ahead = [pltpu.roll(x, LANES - 1, 1) for x in values]
        behind = [pltpu.roll(x, 1, 1) for x in values]
        n = len(values)
        return [
            jnp.where(is_last, ahead[(t + 1) % n], ahead[t]) - jnp.where(is_first, behind[(t - 1) % n], behind[t])
            for t in range(n)
        ]

    def update_stress(vel_in, stress_in, first_row, pieces):
        def body(i, carry):
            start = pl.multiple_of(first_row + i * PIECE, 8)
            rows, above, below = (pl.ds(start + d, PIECE) for d in (0, -1, 1))
            u_x = across([vel_in[0, t, rows, :] for t in tiles])
            v_x = across([vel_in[1, t, rows, :] for t in tiles])
            results = []
            for t in tiles:
                u_y = vel_in[0, t, below, :] - vel_in[0, t, above, :]
                v_y = vel_in[1, t, below, :] - vel_in[1, t, above, :]
                divergence = u_x[t] + v_y
                tension = u_x[t] - v_y
                shearing = u_y + v_x[t]
                inverse = lax.rsqrt(divergence * divergence + 0.25 * (tension * tension + shearing * shearing) + 1.0)
                keep = fixed[0, t, rows, :]
                force = fixed[1, t, rows, :]
                scaled = force * inverse
                quarter = 0.25 * scaled
                results.append((
                    keep * stress_in[0, t, rows, :] + (scaled * divergence - force),
                    keep * stress_in[1, t, rows, :] + quarter * tension,
                    keep * stress_in[2, t, rows, :] + quarter * shearing,
                ))
            for t in tiles:
                for f in range(3):
                    stress[f, t, rows, :] = results[t][f]
            return carry

        lax.fori_loop(0, pieces, body, 0, unroll=UNROLL)

    def update_velocity(vel_in, first_row, pieces):
        def body(i, carry):
            start = pl.multiple_of(first_row + i * PIECE, 8)
            rows, above, below = (pl.ds(start + d, PIECE) for d in (0, -1, 1))
            sum_x = across([stress[0, t, rows, :] + stress[1, t, rows, :] for t in tiles])
            cross_x = across([stress[2, t, rows, :] for t in tiles])
            results = []
            for t in tiles:
                cross_y = stress[2, t, below, :] - stress[2, t, above, :]
                lower = stress[0, t, below, :] - stress[1, t, below, :]
                higher = stress[0, t, above, :] - stress[1, t, above, :]
                mass = fixed[2, t, rows, :]
                rhs_x = mass * vel_in[0, t, rows, :] + (sum_x[t] + cross_y) + fixed[3, t, rows, :]
                rhs_y = mass * vel_in[1, t, rows, :] + (cross_x[t] + (lower - higher)) + fixed[4, t, rows, :]
                ahead = fixed[5, t, rows, :]
                turn = fixed[6, t, rows, :]
                results.append((ahead * rhs_x + turn * rhs_y, ahead * rhs_y - turn * rhs_x))
            for t in tiles:
                for f in range(2):
                    vel[f, t, rows, :] = results[t][f]
            return carry

        lax.fori_loop(0, pieces, body, 0, unroll=UNROLL)

    wide, middle = [(CORE - out, (ROWS + 2 * out) // PIECE) for out in (HALO, HALO // 2)]
    stores = []
    for t in range(TILES):
        stores.append(pltpu.make_async_copy(
            final.at[:, t], stress_out.at[:, :, pl.ds(t * LANES, LANES)], out_sem.at[t]))
    for t in range(TILES):
        stores.append(pltpu.make_async_copy(
            vel.at[:, t, pl.ds(CORE, ROWS), :], vel_out.at[:, :, pl.ds(t * LANES, LANES)],
            out_sem.at[TILES + t]))

    def early(n, carry):
        update_stress(vel, stress, *wide)
        update_velocity(vel, *wide)
        return carry

    def subcycle(n, carry):
        update_stress(vel, stress, *middle)
        update_velocity(vel, *middle)
        return carry

    lax.fori_loop(0, 2, early, 0)
    lax.fori_loop(2, SUB, subcycle, 0)
    for store in stores[TILES:]:
        store.start()
    for t in range(TILES):
        for f, factor in enumerate((4.0, 4.0, 2.0)):
            final[f, t] = factor * stress[f, t, pl.ds(CORE, ROWS), :]
        stores[t].start()
    for store in stores:
        store.wait()


def shards(old_dynamics, old_area, old_volume, old_block, wind_stress, ice_mask):
    owners, subs, pairs = (lax.axis_size(name) for name in ("curve", "sub", "pair"))
    anywhere = pl.BlockSpec(memory_space=pl.ANY)
    real = jnp.float32
    return pl.pallas_call(
        functools.partial(kernel, owners, subs, pairs),
        out_shape=(
            jax.ShapeDtypeStruct((2, ROWS, CB * BS), real),
            jax.ShapeDtypeStruct((3, ROWS, CB * BS), real),
        ),
        in_specs=[anywhere] * 3 + [pl.BlockSpec(memory_space=pltpu.SMEM)] + [anywhere] * 2,
        out_specs=(anywhere, anywhere),
        scratch_shapes=[
            pltpu.VMEM((2, TILES + 1, TALL, LANES), real),
            pltpu.VMEM((3, TILES + 1, TALL, LANES), real),
            pltpu.VMEM((7, TILES + 1, TALL, LANES), real),
            pltpu.VMEM((3, TILES, ROWS, LANES), real),
            pltpu.VMEM((CHUNKS, FIELDS, SLOT, LANES), real),
            pltpu.VMEM((CHUNKS, NCAT, SLOT, LANES), real),
            pltpu.VMEM((CHUNKS, NCAT, SLOT, LANES), real),
            pltpu.VMEM((owners, MOST, FIELDS, CHUNKS, LANES), real),
            pltpu.VMEM((owners, MOST, FIELDS, CHUNKS, LANES), real),
            pltpu.VMEM((10, TILES, TALL, LANES), real),
            pltpu.VMEM((TILES, ROWS, LANES), jnp.int32),
            pltpu.VMEM((2, ROWS, LANES), real),
            pltpu.VMEM((2, SPAN, LANES), real),
            pltpu.SMEM((SLOT,), jnp.int32),
            pltpu.SemaphoreType.DMA((2 * TILES + 3 * CHUNKS,)),
            pltpu.SemaphoreType.DMA((2 * TILES,)),
            pltpu.SemaphoreType.DMA((owners,)),
            pltpu.SemaphoreType.DMA((owners,)),
            pltpu.SemaphoreType.DMA((10,)),
            pltpu.SemaphoreType.DMA((10,)),
        ],
        compiler_params=pltpu.CompilerParams(
            collective_id=0, has_side_effects=True, vmem_limit_bytes=LIMIT * 1024 * 1024
        ),
    )(old_dynamics, old_area, old_volume, old_block, wind_stress, ice_mask)


def solution(mesh):
    return jax.shard_map(
        shards,
        mesh=mesh,
        in_specs=(
            P("groups", "curve", ("sub", "pair")),
            P("groups", "curve", ("sub", "pair")),
            P("groups", "curve", ("sub", "pair")),
            P(),
            P(None, ("groups", "curve"), ("sub", "pair")),
            P(("groups", "curve"), ("sub", "pair")),
        ),
        out_specs=(
            P(None, ("groups", "curve"), ("sub", "pair")),
            P(None, ("groups", "curve"), ("sub", "pair")),
        ),
        check_vma=False,
    )
```

```python
import functools

import jax
import jax.numpy as jnp
from jax import lax
from jax.experimental import pallas as pl
from jax.experimental.pallas import tpu as pltpu
from jax.sharding import PartitionSpec as P

BS = 32
RB = 4
CB = 8
NCAT = 5
SUB = 6
MOST = 2
SLOT = RB * CB
LANES = 128
ROWS = RB * BS
TILES = CB * BS // LANES
CHUNKS = BS * BS // LANES
PER = LANES // BS
WIDE = 2 * SUB
HALO = 16
DEEP = 12
TOP = 8
CORE = TOP + HALO
LOW = CORE + ROWS
TALL = LOW + HALO + 8
SPAN = ROWS + 2 * HALO
STEP = 32
PIECE = 16
UNROLL = True
LIMIT = 56
FIELDS = 7
MESH = pl.DeviceIdType.MESH


def kernel(
    owners, subs, pairs,
    dyn_ref, area_ref, vol_ref, block_ref, wind_ref, mask_ref,
    vel_out, stress_out,
    vel_ref, stress_ref, fixed_ref, final, own, area, vol, send, came, grid, mask, edge, side, source,
    in_sem, out_sem, mig_send, mig_recv, halo_send, halo_recv,
):
    me = lax.axis_index("curve")
    col = lax.axis_index("sub") * pairs + lax.axis_index("pair")
    cols = subs * pairs
    has_up, has_down = me > 0, me < owners - 1
    has_left, has_right = col > 0, col < cols - 1

    def device(d_row, d_col):
        there = lax.rem(col + d_col + cols, cols)
        return {
            "curve": lax.rem(me + d_row + owners, owners),
            "sub": lax.div(there, pairs),
            "pair": lax.rem(there, pairs),
        }

    def exists(d_row, d_col):
        flag = None
        for step, low, high in ((d_row, has_up, has_down), (d_col, has_left, has_right)):
            if step:
                part = low if step < 0 else high
                flag = part if flag is None else jnp.logical_and(flag, part)
        return flag

    loads = []
    for t in range(TILES):
        loads.append(pltpu.make_async_copy(
            wind_ref.at[:, :, pl.ds(t * LANES, LANES)],
            grid.at[pl.ds(FIELDS, 2), t, pl.ds(CORE, ROWS), :], in_sem.at[2 * t]))
        loads.append(pltpu.make_async_copy(
            mask_ref.at[:, pl.ds(t * LANES, LANES)], mask.at[t], in_sem.at[2 * t + 1]))
    base = 2 * TILES
    for j in range(CHUNKS):
        lanes = pl.ds(j * LANES, LANES)
        loads.append(pltpu.make_async_copy(area_ref.at[:, :, lanes], area.at[j], in_sem.at[base + 3 * j]))
        loads.append(pltpu.make_async_copy(vol_ref.at[:, :, lanes], vol.at[j], in_sem.at[base + 3 * j + 1]))
        loads.append(pltpu.make_async_copy(
            dyn_ref.at[:, :, lanes], own.at[j, pl.ds(0, 5)], in_sem.at[base + 3 * j + 2]))
    for load in loads:
        load.start()

    rim = jnp.zeros((10, TILES, CORE, LANES), jnp.float32)
    grid[:, :, pl.ds(0, CORE), :] = rim
    grid[:, :, pl.ds(LOW, CORE), :] = rim
    for ref in (vel_ref, stress_ref):
        pad = jnp.zeros((ref.shape[0], TILES + 1, TOP, LANES), jnp.float32)
        ref[:, :, pl.ds(0, TOP), :] = pad
        ref[:, :, pl.ds(TALL - TOP, TOP), :] = pad
    side[...] = jnp.zeros(side.shape, jnp.float32)

    barrier = pltpu.get_barrier_semaphore()

    def greet(k, carry):
        pl.semaphore_signal(barrier, inc=1, device_id={"curve": lax.rem(me + k, owners)}, device_id_type=MESH)
        return carry

    lax.fori_loop(1, owners, greet, 0)
    count = owners - 1
    around = [(0, -1), (0, 1), (-1, -1), (-1, 1), (1, -1), (1, 1)]
    for d_row, d_col in around:
        flag = exists(d_row, d_col)
        count = count + flag.astype(jnp.int32)

        @pl.when(flag)
        def _():
            pl.semaphore_signal(barrier, inc=1, device_id=device(d_row, d_col), device_id_type=MESH)

    for load in loads[base:]:
        load.wait()

    def derive(j, carry):
        total_area = area[j, 0]
        total_volume = vol[j, 0]
        for n in range(1, NCAT):
            total_area = total_area + area[j, n]
            total_volume = total_volume + vol[j, n]
        own[j, 5] = 2.0 * total_volume * jnp.exp(-2.0 * (1.0 - total_area))
        own[j, 6] = total_volume
        return carry

    lax.fori_loop(0, CHUNKS, derive, 0)

    flat = own.reshape(CHUNKS * FIELDS * SLOT, LANES)

    def block_rows(field, slot):
        return flat[pl.ds(field * SLOT + slot, CHUNKS, stride=FIELDS * SLOT), :]

    def migrate(k):
        to = lax.rem(me + k, owners)
        return pltpu.make_async_remote_copy(
            src_ref=send.at[k], dst_ref=came.at[k],
            send_sem=mig_send.at[k], recv_sem=mig_recv.at[k],
            device_id={"curve": to}, device_id_type=MESH)

    def pack(k, carry):
        to = lax.rem(me + k, owners)
        first, last = jnp.int32(SLOT - 1), jnp.int32(0)
        for s in range(SLOT):
            place = block_ref[me * SLOT + s] - to * SLOT
            match = jnp.logical_and(place >= 0, place < SLOT)
            first = jnp.where(match, jnp.minimum(first, s), first)
            last = jnp.where(match, s, last)
        for rank, slot in enumerate((first, last)):
            for f in range(FIELDS):
                send[k, rank, f] = block_rows(f, slot)
        return carry

    lax.fori_loop(1, owners, pack, 0)
    pl.semaphore_wait(barrier, count)

    def depart(k, carry):
        migrate(k).start()
        return carry

    lax.fori_loop(1, owners, depart, 0)

    for load in loads[:base]:
        load.wait()
    grid[9, pl.ds(0, TILES), pl.ds(CORE, ROWS), :] = mask[...].astype(jnp.float32)

    def row_copy(d_row, start, length, slot):
        here = CORE if d_row < 0 else LOW - DEEP
        there = LOW if d_row < 0 else CORE - DEEP
        return pltpu.make_async_remote_copy(
            src_ref=grid.at[pl.ds(start, length), pl.ds(0, TILES), pl.ds(here, DEEP), :],
            dst_ref=grid.at[pl.ds(start, length), pl.ds(0, TILES), pl.ds(there, DEEP), :],
            send_sem=halo_send.at[slot], recv_sem=halo_recv.at[slot],
            device_id=device(d_row, 0), device_id_type=MESH)

    def each(copies, act):
        for flag, copy in copies:
            @pl.when(flag)
            def _():
                act(copy)

    early = [(exists(-1, 0), row_copy(-1, FIELDS, 3, 0)), (exists(1, 0), row_copy(1, FIELDS, 3, 1))]
    early_back = [(exists(1, 0), early[0][1]), (exists(-1, 0), early[1][1])]
    each(early, lambda copy: copy.start())

    for p in range(SLOT):
        source[p] = jnp.int32(-1)

    def find(k, carry):
        giver = lax.rem(me + owners - k, owners)
        rank = jnp.int32(0)
        for p in range(SLOT):
            place = block_ref[giver * SLOT + p] - me * SLOT
            match = jnp.logical_and(place >= 0, place < SLOT)
            source[p] = jnp.where(match, k * MOST + jnp.minimum(rank, MOST - 1), source[p])
            rank = jnp.where(match, rank + 1, rank)
        return carry

    lax.fori_loop(1, owners, find, 0)

    def arrive(k, carry):
        migrate(k).wait_recv()
        return carry

    lax.fori_loop(1, owners, arrive, 0)

    lane = lax.broadcasted_iota(jnp.int32, (CHUNKS, LANES), 1)
    upper = lane >= LANES // 2
    odd = lax.rem(lax.div(lane, BS), 2) == 1
    arrivals = came.reshape(owners * MOST, FIELDS, CHUNKS, LANES)

    def settle(r, carry):
        for h in range(TILES):
            slots = []
            for m in range(PER):
                p = r * CB + h * PER + m
                here = source[p]
                slots.append((p, here >= 0, jnp.maximum(here, MOST)))
            for f in range(FIELDS):
                v0, v1, v2, v3 = [
                    jnp.where(new, arrivals[index, f], block_rows(f, p)) for p, new, index in slots
                ]
                a0 = jnp.where(upper, pltpu.roll(v2, 64, 1), v0)
                a2 = jnp.where(upper, v2, pltpu.roll(v0, 64, 1))
                a1 = jnp.where(upper, pltpu.roll(v3, 64, 1), v1)
                a3 = jnp.where(upper, v3, pltpu.roll(v1, 64, 1))
                rows = (
                    jnp.where(odd, pltpu.roll(a1, 32, 1), a0),
                    jnp.where(odd, a1, pltpu.roll(a0, 96, 1)),
                    jnp.where(odd, pltpu.roll(a3, 32, 1), a2),
                    jnp.where(odd, a3, pltpu.roll(a2, 96, 1)),
                )
                for y, value in enumerate(rows):
                    grid[f, h, pl.ds(CORE + r * BS + y, CHUNKS, stride=PER), :] = value
        return carry

    lax.fori_loop(0, RB, settle, 0)

    late = [(exists(-1, 0), row_copy(-1, 0, FIELDS, 2)), (exists(1, 0), row_copy(1, 0, FIELDS, 3))]
    late_back = [(exists(1, 0), late[0][1]), (exists(-1, 0), late[1][1])]
    each(late, lambda copy: copy.start())

    def strips(i, carry):
        start = pl.multiple_of(i * STEP, 8)
        place = lax.broadcasted_iota(jnp.int32, (STEP, LANES), 1)
        left = jnp.zeros((STEP, LANES), jnp.float32)
        right = jnp.zeros((STEP, LANES), jnp.float32)
        for f in range(10):
            inside = jnp.logical_and(place >= f * WIDE, place < (f + 1) * WIDE)
            first = grid[f, 0, pl.ds(CORE + start, STEP), :]
            last = grid[f, TILES - 1, pl.ds(CORE + start, STEP), :]
            if f:
                first = pltpu.roll(first, f * WIDE, 1)
            left = jnp.where(inside, first, left)
            right = jnp.where(inside, pltpu.roll(last, ((f + 1) * WIDE) % LANES, 1), right)
        edge[0, pl.ds(start, STEP), :] = left
        edge[1, pl.ds(start, STEP), :] = right
        return carry

    lax.fori_loop(0, ROWS // STEP, strips, 0)

    def strip_copy(d_row, d_col, slot):
        which = 0 if d_col < 0 else 1
        here, length, there = {
            0: (0, ROWS, HALO), -1: (0, DEEP, HALO + ROWS), 1: (ROWS - DEEP, DEEP, HALO - DEEP),
        }[d_row]
        return pltpu.make_async_remote_copy(
            src_ref=edge.at[which, pl.ds(here, length), :],
            dst_ref=side.at[which, pl.ds(there, length), :],
            send_sem=halo_send.at[slot], recv_sem=halo_recv.at[slot],
            device_id=device(d_row, d_col), device_id_type=MESH)

    columns, columns_back = [], []
    for i, (d_row, d_col) in enumerate(around):
        copy = strip_copy(d_row, d_col, 4 + i)
        columns.append((exists(d_row, d_col), copy))
        columns_back.append((exists(-d_row, -d_col), copy))
    each(columns, lambda copy: copy.start())
    def prepare(t, rows, values):
        u, v, s1, s2, s12, strength, mass, wind_x, wind_y, active = values
        drag = mass + 0.5
        turning = 0.5 * mass
        scale = active / (drag * drag + turning * turning)
        keep = active * (1.0 / 1.5)
        vel_ref[0, t, rows, :] = u
        vel_ref[1, t, rows, :] = v
        stress_ref[0, t, rows, :] = 0.25 * s1
        stress_ref[1, t, rows, :] = 0.25 * s2
        stress_ref[2, t, rows, :] = 0.5 * s12
        fixed_ref[0, t, rows, :] = keep
        fixed_ref[1, t, rows, :] = 0.125 * keep * strength
        fixed_ref[2, t, rows, :] = mass
        fixed_ref[3, t, rows, :] = wind_x
        fixed_ref[4, t, rows, :] = wind_y
        fixed_ref[5, t, rows, :] = scale * drag
        fixed_ref[6, t, rows, :] = scale * turning

    def interior(i, carry):
        rows = pl.ds(pl.multiple_of(CORE + i * STEP, 8), STEP)
        for t in range(TILES):
            prepare(t, rows, [grid[f, t, rows, :] for f in range(10)])
        return carry

    lax.fori_loop(0, ROWS // STEP, interior, 0)
    each(early_back + late_back + columns_back, lambda copy: copy.wait_recv())
    for t in range(TILES):
        for start in (TOP, LOW):
            rows = pl.ds(start, HALO)
            prepare(t, rows, [grid[f, t, rows, :] for f in range(10)])

    def spread(i, carry):
        start = pl.multiple_of(i * STEP, 8)
        place = lax.broadcasted_iota(jnp.int32, (STEP, LANES), 1)
        from_right = side[0, pl.ds(start, STEP), :]
        from_left = side[1, pl.ds(start, STEP), :]
        rows = pl.ds(TOP + start, STEP)
        values = []
        for f in range(10):
            first = pltpu.roll(from_right, (LANES - f * WIDE) % LANES, 1) if f else from_right
            last = pltpu.roll(from_left, LANES - (f + 1) * WIDE, 1)
            beyond = jnp.where(place < WIDE, first, jnp.where(place >= LANES - WIDE, last, 0.0))
            values.append(beyond)
        prepare(TILES, rows, values)
        return carry

    lax.fori_loop(0, SPAN // STEP, spread, 0)

    cycles(vel_out, stress_out, vel_ref, stress_ref, fixed_ref, final, out_sem)

    def sent(k, carry):
        migrate(k).wait_send()
        return carry

    lax.fori_loop(1, owners, sent, 0)
    each(early + late + columns, lambda copy: copy.wait_send())


def cycles(vel_out, stress_out, vel, stress, fixed, final, out_sem):
    tiles = range(TILES + 1)
    place = lax.broadcasted_iota(jnp.int32, (PIECE, LANES), 1)
    is_first, is_last = place == 0, place == LANES - 1

    def across(values):
        ahead = [pltpu.roll(x, LANES - 1, 1) for x in values]
        behind = [pltpu.roll(x, 1, 1) for x in values]
        n = len(values)
        return [
            jnp.where(is_last, ahead[(t + 1) % n], ahead[t]) - jnp.where(is_first, behind[(t - 1) % n], behind[t])
            for t in range(n)
        ]

    def update_stress(vel_in, stress_in, first_row, pieces):
        def body(i, carry):
            start = pl.multiple_of(first_row + i * PIECE, 8)
            rows, above, below = (pl.ds(start + d, PIECE) for d in (0, -1, 1))
            u_x = across([vel_in[0, t, rows, :] for t in tiles])
            v_x = across([vel_in[1, t, rows, :] for t in tiles])
            results = []
            for t in tiles:
                u_y = vel_in[0, t, below, :] - vel_in[0, t, above, :]
                v_y = vel_in[1, t, below, :] - vel_in[1, t, above, :]
                divergence = u_x[t] + v_y
                tension = u_x[t] - v_y
                shearing = u_y + v_x[t]
                inverse = lax.rsqrt(divergence * divergence + 0.25 * (tension * tension + shearing * shearing) + 1.0)
                keep = fixed[0, t, rows, :]
                force = fixed[1, t, rows, :]
                scaled = force * inverse
                quarter = 0.25 * scaled
                results.append((
                    keep * stress_in[0, t, rows, :] + (scaled * divergence - force),
                    keep * stress_in[1, t, rows, :] + quarter * tension,
                    keep * stress_in[2, t, rows, :] + quarter * shearing,
                ))
            for t in tiles:
                for f in range(3):
                    stress[f, t, rows, :] = results[t][f]
            return carry

        lax.fori_loop(0, pieces, body, 0, unroll=UNROLL)

    def update_velocity(vel_in, first_row, pieces):
        def body(i, carry):
            start = pl.multiple_of(first_row + i * PIECE, 8)
            rows, above, below = (pl.ds(start + d, PIECE) for d in (0, -1, 1))
            sum_x = across([stress[0, t, rows, :] + stress[1, t, rows, :] for t in tiles])
            cross_x = across([stress[2, t, rows, :] for t in tiles])
            results = []
            for t in tiles:
                cross_y = stress[2, t, below, :] - stress[2, t, above, :]
                lower = stress[0, t, below, :] - stress[1, t, below, :]
                higher = stress[0, t, above, :] - stress[1, t, above, :]
                mass = fixed[2, t, rows, :]
                rhs_x = mass * vel_in[0, t, rows, :] + (sum_x[t] + cross_y) + fixed[3, t, rows, :]
                rhs_y = mass * vel_in[1, t, rows, :] + (cross_x[t] + (lower - higher)) + fixed[4, t, rows, :]
                ahead = fixed[5, t, rows, :]
                turn = fixed[6, t, rows, :]
                results.append((ahead * rhs_x + turn * rhs_y, ahead * rhs_y - turn * rhs_x))
            for t in tiles:
                for f in range(2):
                    vel[f, t, rows, :] = results[t][f]
            return carry

        lax.fori_loop(0, pieces, body, 0, unroll=UNROLL)

    wide, middle = [(CORE - out, (ROWS + 2 * out) // PIECE) for out in (HALO, HALO // 2)]
    stores = []
    for t in range(TILES):
        stores.append(pltpu.make_async_copy(
            final.at[:, t], stress_out.at[:, :, pl.ds(t * LANES, LANES)], out_sem.at[t]))
    for t in range(TILES):
        stores.append(pltpu.make_async_copy(
            vel.at[:, t, pl.ds(CORE, ROWS), :], vel_out.at[:, :, pl.ds(t * LANES, LANES)],
            out_sem.at[TILES + t]))

    def early(n, carry):
        update_stress(vel, stress, *wide)
        update_velocity(vel, *wide)
        return carry

    def subcycle(n, carry):
        update_stress(vel, stress, *middle)
        update_velocity(vel, *middle)
        return carry

    lax.fori_loop(0, 2, early, 0)
    lax.fori_loop(2, SUB, subcycle, 0)
    for store in stores[TILES:]:
        store.start()
    for t in range(TILES):
        for f, factor in enumerate((4.0, 4.0, 2.0)):
            final[f, t] = factor * stress[f, t, pl.ds(CORE, ROWS), :]
        stores[t].start()
    for store in stores:
        store.wait()


def shards(old_dynamics, old_area, old_volume, old_block, wind_stress, ice_mask):
    owners, subs, pairs = (lax.axis_size(name) for name in ("curve", "sub", "pair"))
    anywhere = pl.BlockSpec(memory_space=pl.ANY)
    real = jnp.float32
    return pl.pallas_call(
        functools.partial(kernel, owners, subs, pairs),
        out_shape=(
            jax.ShapeDtypeStruct((2, ROWS, CB * BS), real),
            jax.ShapeDtypeStruct((3, ROWS, CB * BS), real),
        ),
        in_specs=[anywhere] * 3 + [pl.BlockSpec(memory_space=pltpu.SMEM)] + [anywhere] * 2,
        out_specs=(anywhere, anywhere),
        scratch_shapes=[
            pltpu.VMEM((2, TILES + 1, TALL, LANES), real),
            pltpu.VMEM((3, TILES + 1, TALL, LANES), real),
            pltpu.VMEM((7, TILES + 1, TALL, LANES), real),
            pltpu.VMEM((3, TILES, ROWS, LANES), real),
            pltpu.VMEM((CHUNKS, FIELDS, SLOT, LANES), real),
            pltpu.VMEM((CHUNKS, NCAT, SLOT, LANES), real),
            pltpu.VMEM((CHUNKS, NCAT, SLOT, LANES), real),
            pltpu.VMEM((owners, MOST, FIELDS, CHUNKS, LANES), real),
            pltpu.VMEM((owners, MOST, FIELDS, CHUNKS, LANES), real),
            pltpu.VMEM((10, TILES, TALL, LANES), real),
            pltpu.VMEM((TILES, ROWS, LANES), jnp.int32),
            pltpu.VMEM((2, ROWS, LANES), real),
            pltpu.VMEM((2, SPAN, LANES), real),
            pltpu.SMEM((SLOT,), jnp.int32),
            pltpu.SemaphoreType.DMA((2 * TILES + 3 * CHUNKS,)),
            pltpu.SemaphoreType.DMA((2 * TILES,)),
            pltpu.SemaphoreType.DMA((owners,)),
            pltpu.SemaphoreType.DMA((owners,)),
            pltpu.SemaphoreType.DMA((10,)),
            pltpu.SemaphoreType.DMA((10,)),
        ],
        compiler_params=pltpu.CompilerParams(
            collective_id=0, has_side_effects=True, vmem_limit_bytes=LIMIT * 1024 * 1024
        ),
    )(old_dynamics, old_area, old_volume, old_block, wind_stress, ice_mask)


def solution(mesh):
    return jax.shard_map(
        shards,
        mesh=mesh,
        in_specs=(
            P("groups", "curve", ("sub", "pair")),
            P("groups", "curve", ("sub", "pair")),
            P("groups", "curve", ("sub", "pair")),
            P(),
            P(None, ("groups", "curve"), ("sub", "pair")),
            P(("groups", "curve"), ("sub", "pair")),
        ),
        out_specs=(
            P(None, ("groups", "curve"), ("sub", "pair")),
            P(None, ("groups", "curve"), ("sub", "pair")),
        ),
        check_vma=False,
    )
```

```python
import functools

import jax
import jax.numpy as jnp
from jax import lax
from jax.experimental import pallas as pl
from jax.experimental.pallas import tpu as pltpu
from jax.sharding import PartitionSpec as P

BS = 32
RB = 4
CB = 8
NCAT = 5
SUB = 6
MOST = 2
SLOT = RB * CB
LANES = 128
ROWS = RB * BS
TILES = CB * BS // LANES
CHUNKS = BS * BS // LANES
PER = LANES // BS
WIDE = 2 * SUB
HALO = 16
DEEP = 12
TOP = 8
CORE = TOP + HALO
LOW = CORE + ROWS
TALL = LOW + HALO + 8
SPAN = ROWS + 2 * HALO
STEP = 32
PIECE = 8
UNROLL = True
LIMIT = 56
FIELDS = 7
MESH = pl.DeviceIdType.MESH


def kernel(
    owners, subs, pairs,
    dyn_ref, area_ref, vol_ref, block_ref, wind_ref, mask_ref,
    vel_out, stress_out,
    vel_ref, stress_ref, fixed_ref, own, area, vol, send, came, grid, mask, edge, side, source,
    in_sem, out_sem, mig_send, mig_recv, halo_send, halo_recv,
):
    me = lax.axis_index("curve")
    col = lax.axis_index("sub") * pairs + lax.axis_index("pair")
    cols = subs * pairs
    has_up, has_down = me > 0, me < owners - 1
    has_left, has_right = col > 0, col < cols - 1

    def device(d_row, d_col):
        there = lax.rem(col + d_col + cols, cols)
        return {
            "curve": lax.rem(me + d_row + owners, owners),
            "sub": lax.div(there, pairs),
            "pair": lax.rem(there, pairs),
        }

    def exists(d_row, d_col):
        flag = None
        for step, low, high in ((d_row, has_up, has_down), (d_col, has_left, has_right)):
            if step:
                part = low if step < 0 else high
                flag = part if flag is None else jnp.logical_and(flag, part)
        return flag

    loads = []
    for t in range(TILES):
        loads.append(pltpu.make_async_copy(
            wind_ref.at[:, :, pl.ds(t * LANES, LANES)],
            grid.at[pl.ds(FIELDS, 2), t, pl.ds(CORE, ROWS), :], in_sem.at[2 * t]))
        loads.append(pltpu.make_async_copy(
            mask_ref.at[:, pl.ds(t * LANES, LANES)], mask.at[t], in_sem.at[2 * t + 1]))
    base = 2 * TILES
    for j in range(CHUNKS):
        lanes = pl.ds(j * LANES, LANES)
        loads.append(pltpu.make_async_copy(area_ref.at[:, :, lanes], area.at[j], in_sem.at[base + 3 * j]))
        loads.append(pltpu.make_async_copy(vol_ref.at[:, :, lanes], vol.at[j], in_sem.at[base + 3 * j + 1]))
        loads.append(pltpu.make_async_copy(
            dyn_ref.at[:, :, lanes], own.at[j, pl.ds(0, 5)], in_sem.at[base + 3 * j + 2]))
    for load in loads:
        load.start()

    rim = jnp.zeros((10, TILES, CORE, LANES), jnp.float32)
    grid[:, :, pl.ds(0, CORE), :] = rim
    grid[:, :, pl.ds(LOW, CORE), :] = rim
    for ref in (vel_ref, stress_ref):
        pad = jnp.zeros((ref.shape[0], TILES + 1, TOP, LANES), jnp.float32)
        ref[:, :, pl.ds(0, TOP), :] = pad
        ref[:, :, pl.ds(TALL - TOP, TOP), :] = pad
    side[...] = jnp.zeros(side.shape, jnp.float32)

    barrier = pltpu.get_barrier_semaphore()

    def greet(k, carry):
        pl.semaphore_signal(barrier, inc=1, device_id={"curve": lax.rem(me + k, owners)}, device_id_type=MESH)
        return carry

    lax.fori_loop(1, owners, greet, 0)
    count = owners - 1
    around = [(0, -1), (0, 1), (-1, -1), (-1, 1), (1, -1), (1, 1)]
    for d_row, d_col in around:
        flag = exists(d_row, d_col)
        count = count + flag.astype(jnp.int32)

        @pl.when(flag)
        def _():
            pl.semaphore_signal(barrier, inc=1, device_id=device(d_row, d_col), device_id_type=MESH)

    for load in loads[base:]:
        load.wait()

    def derive(j, carry):
        total_area = area[j, 0]
        total_volume = vol[j, 0]
        for n in range(1, NCAT):
            total_area = total_area + area[j, n]
            total_volume = total_volume + vol[j, n]
        own[j, 5] = 2.0 * total_volume * jnp.exp(-2.0 * (1.0 - total_area))
        own[j, 6] = total_volume
        return carry

    lax.fori_loop(0, CHUNKS, derive, 0)

    flat = own.reshape(CHUNKS * FIELDS * SLOT, LANES)

    def block_rows(field, slot):
        return flat[pl.ds(field * SLOT + slot, CHUNKS, stride=FIELDS * SLOT), :]

    def migrate(k):
        to = lax.rem(me + k, owners)
        return pltpu.make_async_remote_copy(
            src_ref=send.at[k], dst_ref=came.at[k],
            send_sem=mig_send.at[k], recv_sem=mig_recv.at[k],
            device_id={"curve": to}, device_id_type=MESH)

    def pack(k, carry):
        to = lax.rem(me + k, owners)
        first, last = jnp.int32(SLOT - 1), jnp.int32(0)
        for s in range(SLOT):
            place = block_ref[me * SLOT + s] - to * SLOT
            match = jnp.logical_and(place >= 0, place < SLOT)
            first = jnp.where(match, jnp.minimum(first, s), first)
            last = jnp.where(match, s, last)
        for rank, slot in enumerate((first, last)):
            for f in range(FIELDS):
                send[k, rank, f] = block_rows(f, slot)
        return carry

    lax.fori_loop(1, owners, pack, 0)
    pl.semaphore_wait(barrier, count)

    def depart(k, carry):
        migrate(k).start()
        return carry

    lax.fori_loop(1, owners, depart, 0)

    for load in loads[:base]:
        load.wait()
    grid[9, pl.ds(0, TILES), pl.ds(CORE, ROWS), :] = mask[...].astype(jnp.float32)

    def row_copy(d_row, start, length, slot):
        here = CORE if d_row < 0 else LOW - DEEP
        there = LOW if d_row < 0 else CORE - DEEP
        return pltpu.make_async_remote_copy(
            src_ref=grid.at[pl.ds(start, length), pl.ds(0, TILES), pl.ds(here, DEEP), :],
            dst_ref=grid.at[pl.ds(start, length), pl.ds(0, TILES), pl.ds(there, DEEP), :],
            send_sem=halo_send.at[slot], recv_sem=halo_recv.at[slot],
            device_id=device(d_row, 0), device_id_type=MESH)

    def each(copies, act):
        for flag, copy in copies:
            @pl.when(flag)
            def _():
                act(copy)

    early = [(exists(-1, 0), row_copy(-1, FIELDS, 3, 0)), (exists(1, 0), row_copy(1, FIELDS, 3, 1))]
    early_back = [(exists(1, 0), early[0][1]), (exists(-1, 0), early[1][1])]
    each(early, lambda copy: copy.start())

    for p in range(SLOT):
        source[p] = jnp.int32(-1)

    def find(k, carry):
        giver = lax.rem(me + owners - k, owners)
        rank = jnp.int32(0)
        for p in range(SLOT):
            place = block_ref[giver * SLOT + p] - me * SLOT
            match = jnp.logical_and(place >= 0, place < SLOT)
            source[p] = jnp.where(match, k * MOST + jnp.minimum(rank, MOST - 1), source[p])
            rank = jnp.where(match, rank + 1, rank)
        return carry

    lax.fori_loop(1, owners, find, 0)

    def arrive(k, carry):
        migrate(k).wait_recv()
        return carry

    lax.fori_loop(1, owners, arrive, 0)

    lane = lax.broadcasted_iota(jnp.int32, (CHUNKS, LANES), 1)
    upper = lane >= LANES // 2
    odd = lax.rem(lax.div(lane, BS), 2) == 1
    arrivals = came.reshape(owners * MOST, FIELDS, CHUNKS, LANES)

    def settle(i, carry):
        r = lax.rem(i * (RB - 1), RB)
        for h in range(TILES):
            slots = []
            for m in range(PER):
                p = r * CB + h * PER + m
                here = source[p]
                slots.append((p, here >= 0, jnp.maximum(here, MOST)))
            for f in range(FIELDS):
                v0, v1, v2, v3 = [
                    jnp.where(new, arrivals[index, f], block_rows(f, p)) for p, new, index in slots
                ]
                a0 = jnp.where(upper, pltpu.roll(v2, 64, 1), v0)
                a2 = jnp.where(upper, v2, pltpu.roll(v0, 64, 1))
                a1 = jnp.where(upper, pltpu.roll(v3, 64, 1), v1)
                a3 = jnp.where(upper, v3, pltpu.roll(v1, 64, 1))
                rows = (
                    jnp.where(odd, pltpu.roll(a1, 32, 1), a0),
                    jnp.where(odd, a1, pltpu.roll(a0, 96, 1)),
                    jnp.where(odd, pltpu.roll(a3, 32, 1), a2),
                    jnp.where(odd, a3, pltpu.roll(a2, 96, 1)),
                )
                for y, value in enumerate(rows):
                    grid[f, h, pl.ds(CORE + r * BS + y, CHUNKS, stride=PER), :] = value
        return carry

    lax.fori_loop(0, 2, settle, 0)

    late = [(exists(-1, 0), row_copy(-1, 0, FIELDS, 2)), (exists(1, 0), row_copy(1, 0, FIELDS, 3))]
    late_back = [(exists(1, 0), late[0][1]), (exists(-1, 0), late[1][1])]
    each(late, lambda copy: copy.start())
    lax.fori_loop(2, RB, settle, 0)

    def strips(i, carry):
        start = pl.multiple_of(i * STEP, 8)
        place = lax.broadcasted_iota(jnp.int32, (STEP, LANES), 1)
        left = jnp.zeros((STEP, LANES), jnp.float32)
        right = jnp.zeros((STEP, LANES), jnp.float32)
        for f in range(10):
            inside = jnp.logical_and(place >= f * WIDE, place < (f + 1) * WIDE)
            first = grid[f, 0, pl.ds(CORE + start, STEP), :]
            last = grid[f, TILES - 1, pl.ds(CORE + start, STEP), :]
            if f:
                first = pltpu.roll(first, f * WIDE, 1)
            left = jnp.where(inside, first, left)
            right = jnp.where(inside, pltpu.roll(last, ((f + 1) * WIDE) % LANES, 1), right)
        edge[0, pl.ds(start, STEP), :] = left
        edge[1, pl.ds(start, STEP), :] = right
        return carry

    lax.fori_loop(0, ROWS // STEP, strips, 0)

    def strip_copy(d_row, d_col, slot):
        which = 0 if d_col < 0 else 1
        here, length, there = {
            0: (0, ROWS, HALO), -1: (0, DEEP, HALO + ROWS), 1: (ROWS - DEEP, DEEP, HALO - DEEP),
        }[d_row]
        return pltpu.make_async_remote_copy(
            src_ref=edge.at[which, pl.ds(here, length), :],
            dst_ref=side.at[which, pl.ds(there, length), :],
            send_sem=halo_send.at[slot], recv_sem=halo_recv.at[slot],
            device_id=device(d_row, d_col), device_id_type=MESH)

    columns, columns_back = [], []
    for i, (d_row, d_col) in enumerate(around):
        copy = strip_copy(d_row, d_col, 4 + i)
        columns.append((exists(d_row, d_col), copy))
        columns_back.append((exists(-d_row, -d_col), copy))
    each(columns, lambda copy: copy.start())
    def prepare(t, rows, values):
        u, v, s1, s2, s12, strength, mass, wind_x, wind_y, active = values
        drag = mass + 0.5
        turning = 0.5 * mass
        scale = active / (drag * drag + turning * turning)
        keep = active * (1.0 / 1.5)
        vel_ref[0, t, rows, :] = 0.5 * u
        vel_ref[1, t, rows, :] = 0.5 * v
        stress_ref[0, t, rows, :] = 0.125 * s1
        stress_ref[1, t, rows, :] = 0.125 * s2
        stress_ref[2, t, rows, :] = 0.25 * s12
        fixed_ref[0, t, rows, :] = keep
        fixed_ref[1, t, rows, :] = 0.0625 * keep * strength
        fixed_ref[2, t, rows, :] = mass
        fixed_ref[3, t, rows, :] = 0.5 * wind_x
        fixed_ref[4, t, rows, :] = 0.5 * wind_y
        fixed_ref[5, t, rows, :] = scale * drag
        fixed_ref[6, t, rows, :] = scale * turning

    def interior(i, carry):
        rows = pl.ds(pl.multiple_of(CORE + i * STEP, 8), STEP)
        for t in range(TILES):
            prepare(t, rows, [grid[f, t, rows, :] for f in range(10)])
        return carry

    lax.fori_loop(0, ROWS // STEP, interior, 0)
    each(early_back + late_back + columns_back, lambda copy: copy.wait_recv())
    for t in range(TILES):
        for start in (TOP, LOW):
            rows = pl.ds(start, HALO)
            prepare(t, rows, [grid[f, t, rows, :] for f in range(10)])

    def spread(i, carry):
        start = pl.multiple_of(i * STEP, 8)
        place = lax.broadcasted_iota(jnp.int32, (STEP, LANES), 1)
        from_right = side[0, pl.ds(start, STEP), :]
        from_left = side[1, pl.ds(start, STEP), :]
        rows = pl.ds(TOP + start, STEP)
        values = []
        for f in range(10):
            first = pltpu.roll(from_right, (LANES - f * WIDE) % LANES, 1) if f else from_right
            last = pltpu.roll(from_left, LANES - (f + 1) * WIDE, 1)
            beyond = jnp.where(place < WIDE, first, jnp.where(place >= LANES - WIDE, last, 0.0))
            values.append(beyond)
        prepare(TILES, rows, values)
        return carry

    lax.fori_loop(0, SPAN // STEP, spread, 0)

    cycles(vel_out, stress_out, vel_ref, stress_ref, fixed_ref, out_sem)

    def sent(k, carry):
        migrate(k).wait_send()
        return carry

    lax.fori_loop(1, owners, sent, 0)
    each(early + late + columns, lambda copy: copy.wait_send())


def cycles(vel_out, stress_out, vel, stress, fixed, out_sem):
    tiles = range(TILES + 1)
    place = lax.broadcasted_iota(jnp.int32, (PIECE, LANES), 1)
    is_first, is_last = place == 0, place == LANES - 1

    def across(values):
        ahead = [pltpu.roll(x, LANES - 1, 1) for x in values]
        behind = [pltpu.roll(x, 1, 1) for x in values]
        n = len(values)
        return [
            jnp.where(is_last, ahead[(t + 1) % n], ahead[t]) - jnp.where(is_first, behind[(t - 1) % n], behind[t])
            for t in range(n)
        ]

    def update_stress(vel_in, stress_in, first_row, pieces):
        def body(i, carry):
            start = pl.multiple_of(first_row + i * PIECE, 8)
            rows, above, below = (pl.ds(start + d, PIECE) for d in (0, -1, 1))
            u_x = across([vel_in[0, t, rows, :] for t in tiles])
            v_x = across([vel_in[1, t, rows, :] for t in tiles])
            results = []
            for t in tiles:
                u_y = vel_in[0, t, below, :] - vel_in[0, t, above, :]
                v_y = vel_in[1, t, below, :] - vel_in[1, t, above, :]
                divergence = u_x[t] + v_y
                tension = u_x[t] - v_y
                shearing = u_y + v_x[t]
                inverse = lax.rsqrt(divergence * divergence + 0.25 * (tension * tension + shearing * shearing) + 0.25)
                keep = fixed[0, t, rows, :]
                force = fixed[1, t, rows, :]
                scaled = force * inverse
                quarter = 0.25 * scaled
                results.append((
                    keep * stress_in[0, t, rows, :] + (scaled * divergence - force),
                    keep * stress_in[1, t, rows, :] + quarter * tension,
                    keep * stress_in[2, t, rows, :] + quarter * shearing,
                ))
            for t in tiles:
                for f in range(3):
                    stress[f, t, rows, :] = results[t][f]
            return carry

        lax.fori_loop(0, pieces, body, 0, unroll=UNROLL)

    def update_velocity(vel_in, first_row, pieces):
        def body(i, carry):
            start = pl.multiple_of(first_row + i * PIECE, 8)
            rows, above, below = (pl.ds(start + d, PIECE) for d in (0, -1, 1))
            sum_x = across([stress[0, t, rows, :] + stress[1, t, rows, :] for t in tiles])
            cross_x = across([stress[2, t, rows, :] for t in tiles])
            results = []
            for t in tiles:
                cross_y = stress[2, t, below, :] - stress[2, t, above, :]
                lower = stress[0, t, below, :] - stress[1, t, below, :]
                higher = stress[0, t, above, :] - stress[1, t, above, :]
                mass = fixed[2, t, rows, :]
                rhs_x = mass * vel_in[0, t, rows, :] + (sum_x[t] + cross_y) + fixed[3, t, rows, :]
                rhs_y = mass * vel_in[1, t, rows, :] + (cross_x[t] + (lower - higher)) + fixed[4, t, rows, :]
                ahead = fixed[5, t, rows, :]
                turn = fixed[6, t, rows, :]
                results.append((ahead * rhs_x + turn * rhs_y, ahead * rhs_y - turn * rhs_x))
            for t in tiles:
                for f in range(2):
                    vel[f, t, rows, :] = results[t][f]
            return carry

        lax.fori_loop(0, pieces, body, 0, unroll=UNROLL)

    wide, middle = [(CORE - out, (ROWS + 2 * out) // PIECE) for out in (HALO, HALO // 2)]
    stores = []
    for t in range(TILES):
        stores.append(pltpu.make_async_copy(
            stress.at[:, t, pl.ds(CORE, ROWS), :], stress_out.at[:, :, pl.ds(t * LANES, LANES)], out_sem.at[t]))
    for t in range(TILES):
        stores.append(pltpu.make_async_copy(
            vel.at[:, t, pl.ds(CORE, ROWS), :], vel_out.at[:, :, pl.ds(t * LANES, LANES)],
            out_sem.at[TILES + t]))

    def early(n, carry):
        update_stress(vel, stress, *wide)
        update_velocity(vel, *wide)
        return carry

    def subcycle(n, carry):
        update_stress(vel, stress, *middle)
        update_velocity(vel, *middle)
        return carry

    lax.fori_loop(0, 2, early, 0)
    lax.fori_loop(2, SUB, subcycle, 0)
    for store in stores:
        store.start()
    for store in stores:
        store.wait()


def shards(old_dynamics, old_area, old_volume, old_block, wind_stress, ice_mask):
    owners, subs, pairs = (lax.axis_size(name) for name in ("curve", "sub", "pair"))
    anywhere = pl.BlockSpec(memory_space=pl.ANY)
    real = jnp.float32
    velocity, stress = pl.pallas_call(
        functools.partial(kernel, owners, subs, pairs),
        out_shape=(
            jax.ShapeDtypeStruct((2, ROWS, CB * BS), real),
            jax.ShapeDtypeStruct((3, ROWS, CB * BS), real),
        ),
        in_specs=[anywhere] * 3 + [pl.BlockSpec(memory_space=pltpu.SMEM)] + [anywhere] * 2,
        out_specs=(anywhere, anywhere),
        scratch_shapes=[
            pltpu.VMEM((2, TILES + 1, TALL, LANES), real),
            pltpu.VMEM((3, TILES + 1, TALL, LANES), real),
            pltpu.VMEM((7, TILES + 1, TALL, LANES), real),
            pltpu.VMEM((CHUNKS, FIELDS, SLOT, LANES), real),
            pltpu.VMEM((CHUNKS, NCAT, SLOT, LANES), real),
            pltpu.VMEM((CHUNKS, NCAT, SLOT, LANES), real),
            pltpu.VMEM((owners, MOST, FIELDS, CHUNKS, LANES), real),
            pltpu.VMEM((owners, MOST, FIELDS, CHUNKS, LANES), real),
            pltpu.VMEM((10, TILES, TALL, LANES), real),
            pltpu.VMEM((TILES, ROWS, LANES), jnp.int32),
            pltpu.VMEM((2, ROWS, LANES), real),
            pltpu.VMEM((2, SPAN, LANES), real),
            pltpu.SMEM((SLOT,), jnp.int32),
            pltpu.SemaphoreType.DMA((2 * TILES + 3 * CHUNKS,)),
            pltpu.SemaphoreType.DMA((2 * TILES,)),
            pltpu.SemaphoreType.DMA((owners,)),
            pltpu.SemaphoreType.DMA((owners,)),
            pltpu.SemaphoreType.DMA((10,)),
            pltpu.SemaphoreType.DMA((10,)),
        ],
        compiler_params=pltpu.CompilerParams(
            collective_id=0, has_side_effects=True, vmem_limit_bytes=LIMIT * 1024 * 1024
        ),
    )(old_dynamics, old_area, old_volume, old_block, wind_stress, ice_mask)
    factors = jnp.array([8.0, 8.0, 4.0], real).reshape(3, 1, 1)
    return 2.0 * velocity, factors * stress


def solution(mesh):
    return jax.shard_map(
        shards,
        mesh=mesh,
        in_specs=(
            P("groups", "curve", ("sub", "pair")),
            P("groups", "curve", ("sub", "pair")),
            P("groups", "curve", ("sub", "pair")),
            P(),
            P(None, ("groups", "curve"), ("sub", "pair")),
            P(("groups", "curve"), ("sub", "pair")),
        ),
        out_specs=(
            P(None, ("groups", "curve"), ("sub", "pair")),
            P(None, ("groups", "curve"), ("sub", "pair")),
        ),
        check_vma=False,
    )
```

```python
import functools

import jax
import jax.numpy as jnp
from jax import lax
from jax.experimental import pallas as pl
from jax.experimental.pallas import tpu as pltpu
from jax.sharding import PartitionSpec as P

BS = 32
RB = 4
CB = 8
NCAT = 5
SUB = 6
MOST = 2
SLOT = RB * CB
LANES = 128
ROWS = RB * BS
TILES = CB * BS // LANES
CHUNKS = BS * BS // LANES
PER = LANES // BS
WIDE = 2 * SUB
HALO = 16
DEEP = 12
TOP = 8
CORE = TOP + HALO
LOW = CORE + ROWS
TALL = LOW + HALO + 8
SPAN = ROWS + 2 * HALO
STEP = 32
PIECE = 8
UNROLL = True
LIMIT = 56
FIELDS = 7
MESH = pl.DeviceIdType.MESH


def kernel(
    owners, subs, pairs,
    dyn_ref, area_ref, vol_ref, block_ref, wind_ref, mask_ref,
    vel_out, stress_out,
    vel_ref, stress_ref, fixed_ref, own, area, vol, send, came, grid, mask, edge, side, source,
    in_sem, out_sem, mig_send, mig_recv, halo_send, halo_recv,
):
    me = lax.axis_index("curve")
    col = lax.axis_index("sub") * pairs + lax.axis_index("pair")
    cols = subs * pairs
    has_up, has_down = me > 0, me < owners - 1
    has_left, has_right = col > 0, col < cols - 1

    def device(d_row, d_col):
        there = lax.rem(col + d_col + cols, cols)
        return {
            "curve": lax.rem(me + d_row + owners, owners),
            "sub": lax.div(there, pairs),
            "pair": lax.rem(there, pairs),
        }

    def exists(d_row, d_col):
        flag = None
        for step, low, high in ((d_row, has_up, has_down), (d_col, has_left, has_right)):
            if step:
                part = low if step < 0 else high
                flag = part if flag is None else jnp.logical_and(flag, part)
        return flag

    loads = []
    for t in range(TILES):
        loads.append(pltpu.make_async_copy(
            wind_ref.at[:, :, pl.ds(t * LANES, LANES)],
            grid.at[pl.ds(FIELDS, 2), t, pl.ds(CORE, ROWS), :], in_sem.at[2 * t]))
        loads.append(pltpu.make_async_copy(
            mask_ref.at[:, pl.ds(t * LANES, LANES)], mask.at[t], in_sem.at[2 * t + 1]))
    base = 2 * TILES
    for j in range(CHUNKS):
        lanes = pl.ds(j * LANES, LANES)
        loads.append(pltpu.make_async_copy(area_ref.at[:, :, lanes], area.at[j], in_sem.at[base + 3 * j]))
        loads.append(pltpu.make_async_copy(vol_ref.at[:, :, lanes], vol.at[j], in_sem.at[base + 3 * j + 1]))
        loads.append(pltpu.make_async_copy(
            dyn_ref.at[:, :, lanes], own.at[j, pl.ds(0, 5)], in_sem.at[base + 3 * j + 2]))
    for load in loads:
        load.start()

    rim = jnp.zeros((10, TILES, CORE, LANES), jnp.float32)
    grid[:, :, pl.ds(0, CORE), :] = rim
    grid[:, :, pl.ds(LOW, CORE), :] = rim
    for ref in (vel_ref, stress_ref):
        pad = jnp.zeros((ref.shape[0], TILES + 1, TOP, LANES), jnp.float32)
        ref[:, :, pl.ds(0, TOP), :] = pad
        ref[:, :, pl.ds(TALL - TOP, TOP), :] = pad
    side[...] = jnp.zeros(side.shape, jnp.float32)

    barrier = pltpu.get_barrier_semaphore()

    def greet(k, carry):
        pl.semaphore_signal(barrier, inc=1, device_id={"curve": lax.rem(me + k, owners)}, device_id_type=MESH)
        return carry

    lax.fori_loop(1, owners, greet, 0)
    count = owners - 1
    around = [(0, -1), (0, 1), (-1, -1), (-1, 1), (1, -1), (1, 1)]
    for d_row, d_col in around:
        flag = exists(d_row, d_col)
        count = count + flag.astype(jnp.int32)

        @pl.when(flag)
        def _():
            pl.semaphore_signal(barrier, inc=1, device_id=device(d_row, d_col), device_id_type=MESH)

    for load in loads[base:]:
        load.wait()

    def derive(j, carry):
        total_area = area[j, 0]
        total_volume = vol[j, 0]
        for n in range(1, NCAT):
            total_area = total_area + area[j, n]
            total_volume = total_volume + vol[j, n]
        own[j, 5] = 2.0 * total_volume * jnp.exp(-2.0 * (1.0 - total_area))
        own[j, 6] = total_volume
        return carry

    lax.fori_loop(0, CHUNKS, derive, 0)

    flat = own.reshape((CHUNKS + 1) * FIELDS * SLOT, LANES)

    def block_rows(field, slot):
        return flat[pl.ds(field * SLOT + slot, CHUNKS, stride=FIELDS * SLOT), :]

    def migrate(k):
        to = lax.rem(me + k, owners)
        return pltpu.make_async_remote_copy(
            src_ref=send.at[k], dst_ref=came.at[k],
            send_sem=mig_send.at[k], recv_sem=mig_recv.at[k],
            device_id={"curve": to}, device_id_type=MESH)

    def pack(k, carry):
        to = lax.rem(me + k, owners)
        first, last = jnp.int32(SLOT - 1), jnp.int32(0)
        for s in range(SLOT):
            place = block_ref[me * SLOT + s] - to * SLOT
            match = jnp.logical_and(place >= 0, place < SLOT)
            first = jnp.where(match, jnp.minimum(first, s), first)
            last = jnp.where(match, s, last)
        for rank, slot in enumerate((first, last)):
            for f in range(FIELDS):
                send[k, rank, f] = block_rows(f, slot)
        return carry

    lax.fori_loop(1, owners, pack, 0)
    pl.semaphore_wait(barrier, count)

    def depart(k, carry):
        migrate(k).start()
        return carry

    lax.fori_loop(1, owners, depart, 0)

    for load in loads[:base]:
        load.wait()
    grid[9, pl.ds(0, TILES), pl.ds(CORE, ROWS), :] = mask[...].astype(jnp.float32)

    def row_copy(d_row, start, length, slot):
        here = CORE if d_row < 0 else LOW - DEEP
        there = LOW if d_row < 0 else CORE - DEEP
        return pltpu.make_async_remote_copy(
            src_ref=grid.at[pl.ds(start, length), pl.ds(0, TILES), pl.ds(here, DEEP), :],
            dst_ref=grid.at[pl.ds(start, length), pl.ds(0, TILES), pl.ds(there, DEEP), :],
            send_sem=halo_send.at[slot], recv_sem=halo_recv.at[slot],
            device_id=device(d_row, 0), device_id_type=MESH)

    def each(copies, act):
        for flag, copy in copies:
            @pl.when(flag)
            def _():
                act(copy)

    early = [(exists(-1, 0), row_copy(-1, FIELDS, 3, 0)), (exists(1, 0), row_copy(1, FIELDS, 3, 1))]
    early_back = [(exists(1, 0), early[0][1]), (exists(-1, 0), early[1][1])]
    each(early, lambda copy: copy.start())

    for p in range(SLOT):
        source[p] = jnp.int32(-1)

    def find(k, carry):
        giver = lax.rem(me + owners - k, owners)
        rank = jnp.int32(0)
        for p in range(SLOT):
            place = block_ref[giver * SLOT + p] - me * SLOT
            match = jnp.logical_and(place >= 0, place < SLOT)
            source[p] = jnp.where(match, k * MOST + jnp.minimum(rank, MOST - 1), source[p])
            rank = jnp.where(match, rank + 1, rank)
        return carry

    lax.fori_loop(1, owners, find, 0)

    def arrive(k, carry):
        migrate(k).wait_recv()
        return carry

    lax.fori_loop(1, owners, arrive, 0)

    lane = lax.broadcasted_iota(jnp.int32, (CHUNKS, LANES), 1)
    upper = lane >= LANES // 2
    odd = lax.rem(lax.div(lane, BS), 2) == 1
    arrivals = came.reshape(owners * MOST, FIELDS, CHUNKS, LANES)

    def settle(i, carry):
        r = lax.rem(i * (RB - 1), RB)
        for h in range(TILES):
            slots = []
            for m in range(PER):
                p = r * CB + h * PER + m
                here = source[p]
                slots.append((p, here >= 0, jnp.maximum(here, MOST)))
            for f in range(FIELDS):
                v0, v1, v2, v3 = [
                    jnp.where(new, arrivals[index, f], block_rows(f, p)) for p, new, index in slots
                ]
                a0 = jnp.where(upper, pltpu.roll(v2, 64, 1), v0)
                a2 = jnp.where(upper, v2, pltpu.roll(v0, 64, 1))
                a1 = jnp.where(upper, pltpu.roll(v3, 64, 1), v1)
                a3 = jnp.where(upper, v3, pltpu.roll(v1, 64, 1))
                rows = (
                    jnp.where(odd, pltpu.roll(a1, 32, 1), a0),
                    jnp.where(odd, a1, pltpu.roll(a0, 96, 1)),
                    jnp.where(odd, pltpu.roll(a3, 32, 1), a2),
                    jnp.where(odd, a3, pltpu.roll(a2, 96, 1)),
                )
                for y, value in enumerate(rows):
                    grid[f, h, pl.ds(CORE + r * BS + y, CHUNKS, stride=PER), :] = value
        return carry

    lax.fori_loop(0, 2, settle, 0)

    late = [(exists(-1, 0), row_copy(-1, 0, FIELDS, 2)), (exists(1, 0), row_copy(1, 0, FIELDS, 3))]
    late_back = [(exists(1, 0), late[0][1]), (exists(-1, 0), late[1][1])]
    each(late, lambda copy: copy.start())
    lax.fori_loop(2, RB, settle, 0)

    def strips(i, carry):
        start = pl.multiple_of(i * STEP, 8)
        place = lax.broadcasted_iota(jnp.int32, (STEP, LANES), 1)
        left = jnp.zeros((STEP, LANES), jnp.float32)
        right = jnp.zeros((STEP, LANES), jnp.float32)
        for f in range(10):
            inside = jnp.logical_and(place >= f * WIDE, place < (f + 1) * WIDE)
            first = grid[f, 0, pl.ds(CORE + start, STEP), :]
            last = grid[f, TILES - 1, pl.ds(CORE + start, STEP), :]
            if f:
                first = pltpu.roll(first, f * WIDE, 1)
            left = jnp.where(inside, first, left)
            right = jnp.where(inside, pltpu.roll(last, ((f + 1) * WIDE) % LANES, 1), right)
        edge[0, pl.ds(start, STEP), :] = left
        edge[1, pl.ds(start, STEP), :] = right
        return carry

    lax.fori_loop(0, ROWS // STEP, strips, 0)

    def strip_copy(d_row, d_col, slot):
        which = 0 if d_col < 0 else 1
        here, length, there = {
            0: (0, ROWS, HALO), -1: (0, DEEP, HALO + ROWS), 1: (ROWS - DEEP, DEEP, HALO - DEEP),
        }[d_row]
        return pltpu.make_async_remote_copy(
            src_ref=edge.at[which, pl.ds(here, length), :],
            dst_ref=side.at[which, pl.ds(there, length), :],
            send_sem=halo_send.at[slot], recv_sem=halo_recv.at[slot],
            device_id=device(d_row, d_col), device_id_type=MESH)

    columns, columns_back = [], []
    for i, (d_row, d_col) in enumerate(around):
        copy = strip_copy(d_row, d_col, 4 + i)
        columns.append((exists(d_row, d_col), copy))
        columns_back.append((exists(-d_row, -d_col), copy))
    each(columns, lambda copy: copy.start())
    def prepare(t, rows, values):
        u, v, s1, s2, s12, strength, mass, wind_x, wind_y, active = values
        drag = mass + 0.5
        turning = 0.5 * mass
        scale = active / (drag * drag + turning * turning)
        keep = active * (1.0 / 1.5)
        vel_ref[0, t, rows, :] = 0.5 * u
        vel_ref[1, t, rows, :] = 0.5 * v
        stress_ref[0, t, rows, :] = 0.125 * s1
        stress_ref[1, t, rows, :] = 0.125 * s2
        stress_ref[2, t, rows, :] = 0.25 * s12
        fixed_ref[0, t, rows, :] = keep
        fixed_ref[1, t, rows, :] = 0.0625 * keep * strength
        fixed_ref[2, t, rows, :] = mass
        fixed_ref[3, t, rows, :] = 0.5 * wind_x
        fixed_ref[4, t, rows, :] = 0.5 * wind_y
        fixed_ref[5, t, rows, :] = scale * drag
        fixed_ref[6, t, rows, :] = scale * turning

    def interior(i, carry):
        rows = pl.ds(pl.multiple_of(CORE + i * STEP, 8), STEP)
        for t in range(TILES):
            prepare(t, rows, [grid[f, t, rows, :] for f in range(10)])
        return carry

    lax.fori_loop(0, ROWS // STEP, interior, 0)
    each(early_back + late_back + columns_back, lambda copy: copy.wait_recv())
    for t in range(TILES):
        for start in (TOP, LOW):
            rows = pl.ds(start, HALO)
            prepare(t, rows, [grid[f, t, rows, :] for f in range(10)])

    def spread(i, carry):
        start = pl.multiple_of(i * STEP, 8)
        place = lax.broadcasted_iota(jnp.int32, (STEP, LANES), 1)
        from_right = side[0, pl.ds(start, STEP), :]
        from_left = side[1, pl.ds(start, STEP), :]
        rows = pl.ds(TOP + start, STEP)
        values = []
        for f in range(10):
            first = pltpu.roll(from_right, (LANES - f * WIDE) % LANES, 1) if f else from_right
            last = pltpu.roll(from_left, LANES - (f + 1) * WIDE, 1)
            beyond = jnp.where(place < WIDE, first, jnp.where(place >= LANES - WIDE, last, 0.0))
            values.append(beyond)
        prepare(TILES, rows, values)
        return carry

    lax.fori_loop(0, SPAN // STEP, spread, 0)

    cycles(vel_out, stress_out, vel_ref, stress_ref, fixed_ref, out_sem)

    def sent(k, carry):
        migrate(k).wait_send()
        return carry

    lax.fori_loop(1, owners, sent, 0)
    each(early + late + columns, lambda copy: copy.wait_send())


def cycles(vel_out, stress_out, vel, stress, fixed, out_sem):
    tiles = range(TILES + 1)
    place = lax.broadcasted_iota(jnp.int32, (PIECE, LANES), 1)
    is_first, is_last = place == 0, place == LANES - 1

    def across(values):
        ahead = [pltpu.roll(x, LANES - 1, 1) for x in values]
        behind = [pltpu.roll(x, 1, 1) for x in values]
        n = len(values)
        return [
            jnp.where(is_last, ahead[(t + 1) % n], ahead[t]) - jnp.where(is_first, behind[(t - 1) % n], behind[t])
            for t in range(n)
        ]

    def update_stress(vel_in, stress_in, first_row, pieces):
        def body(i, carry):
            start = pl.multiple_of(first_row + i * PIECE, 8)
            rows, above, below = (pl.ds(start + d, PIECE) for d in (0, -1, 1))
            u_x = across([vel_in[0, t, rows, :] for t in tiles])
            v_x = across([vel_in[1, t, rows, :] for t in tiles])
            results = []
            for t in tiles:
                u_y = vel_in[0, t, below, :] - vel_in[0, t, above, :]
                v_y = vel_in[1, t, below, :] - vel_in[1, t, above, :]
                divergence = u_x[t] + v_y
                tension = u_x[t] - v_y
                shearing = u_y + v_x[t]
                inverse = lax.rsqrt(divergence * divergence + 0.25 * (tension * tension + shearing * shearing) + 0.25)
                keep = fixed[0, t, rows, :]
                force = fixed[1, t, rows, :]
                scaled = force * inverse
                quarter = 0.25 * scaled
                results.append((
                    keep * stress_in[0, t, rows, :] + (scaled * divergence - force),
                    keep * stress_in[1, t, rows, :] + quarter * tension,
                    keep * stress_in[2, t, rows, :] + quarter * shearing,
                ))
            for t in tiles:
                for f in range(3):
                    stress[f, t, rows, :] = results[t][f]
            return carry

        lax.fori_loop(0, pieces, body, 0, unroll=UNROLL)

    def update_velocity(vel_in, first_row, pieces):
        def body(i, carry):
            start = pl.multiple_of(first_row + i * PIECE, 8)
            rows, above, below = (pl.ds(start + d, PIECE) for d in (0, -1, 1))
            sum_x = across([stress[0, t, rows, :] + stress[1, t, rows, :] for t in tiles])
            cross_x = across([stress[2, t, rows, :] for t in tiles])
            results = []
            for t in tiles:
                cross_y = stress[2, t, below, :] - stress[2, t, above, :]
                lower = stress[0, t, below, :] - stress[1, t, below, :]
                higher = stress[0, t, above, :] - stress[1, t, above, :]
                mass = fixed[2, t, rows, :]
                rhs_x = mass * vel_in[0, t, rows, :] + (sum_x[t] + cross_y) + fixed[3, t, rows, :]
                rhs_y = mass * vel_in[1, t, rows, :] + (cross_x[t] + (lower - higher)) + fixed[4, t, rows, :]
                ahead = fixed[5, t, rows, :]
                turn = fixed[6, t, rows, :]
                results.append((ahead * rhs_x + turn * rhs_y, ahead * rhs_y - turn * rhs_x))
            for t in tiles:
                for f in range(2):
                    vel[f, t, rows, :] = results[t][f]
            return carry

        lax.fori_loop(0, pieces, body, 0, unroll=UNROLL)

    wide, middle = [(CORE - out, (ROWS + 2 * out) // PIECE) for out in (HALO, HALO // 2)]
    stores = []
    for t in range(TILES):
        stores.append(pltpu.make_async_copy(
            stress.at[:, t, pl.ds(CORE, ROWS), :], stress_out.at[:, :, pl.ds(t * LANES, LANES)], out_sem.at[t]))
    for t in range(TILES):
        stores.append(pltpu.make_async_copy(
            vel.at[:, t, pl.ds(CORE, ROWS), :], vel_out.at[:, :, pl.ds(t * LANES, LANES)],
            out_sem.at[TILES + t]))

    def early(n, carry):
        update_stress(vel, stress, *wide)
        update_velocity(vel, *wide)
        return carry

    def subcycle(n, carry):
        update_stress(vel, stress, *middle)
        update_velocity(vel, *middle)
        return carry

    lax.fori_loop(0, 2, early, 0)
    lax.fori_loop(2, SUB, subcycle, 0)
    for store in stores:
        store.start()
    for store in stores:
        store.wait()


def shards(old_dynamics, old_area, old_volume, old_block, wind_stress, ice_mask):
    owners, subs, pairs = (lax.axis_size(name) for name in ("curve", "sub", "pair"))
    anywhere = pl.BlockSpec(memory_space=pl.ANY)
    real = jnp.float32
    velocity, stress = pl.pallas_call(
        functools.partial(kernel, owners, subs, pairs),
        out_shape=(
            jax.ShapeDtypeStruct((2, ROWS, CB * BS), real),
            jax.ShapeDtypeStruct((3, ROWS, CB * BS), real),
        ),
        in_specs=[anywhere] * 3 + [pl.BlockSpec(memory_space=pltpu.SMEM)] + [anywhere] * 2,
        out_specs=(anywhere, anywhere),
        scratch_shapes=[
            pltpu.VMEM((2, TILES + 1, TALL, LANES), real),
            pltpu.VMEM((3, TILES + 1, TALL, LANES), real),
            pltpu.VMEM((7, TILES + 1, TALL, LANES), real),
            pltpu.VMEM((CHUNKS + 1, FIELDS, SLOT, LANES), real),
            pltpu.VMEM((CHUNKS, NCAT, SLOT, LANES), real),
            pltpu.VMEM((CHUNKS, NCAT, SLOT, LANES), real),
            pltpu.VMEM((owners, MOST, FIELDS, CHUNKS, LANES), real),
            pltpu.VMEM((owners, MOST, FIELDS, CHUNKS, LANES), real),
            pltpu.VMEM((10, TILES, TALL, LANES), real),
            pltpu.VMEM((TILES, ROWS, LANES), jnp.int32),
            pltpu.VMEM((2, ROWS, LANES), real),
            pltpu.VMEM((2, SPAN, LANES), real),
            pltpu.SMEM((SLOT,), jnp.int32),
            pltpu.SemaphoreType.DMA((2 * TILES + 3 * CHUNKS,)),
            pltpu.SemaphoreType.DMA((2 * TILES,)),
            pltpu.SemaphoreType.DMA((owners,)),
            pltpu.SemaphoreType.DMA((owners,)),
            pltpu.SemaphoreType.DMA((10,)),
            pltpu.SemaphoreType.DMA((10,)),
        ],
        compiler_params=pltpu.CompilerParams(
            collective_id=0, has_side_effects=True, vmem_limit_bytes=LIMIT * 1024 * 1024
        ),
    )(old_dynamics, old_area, old_volume, old_block, wind_stress, ice_mask)
    factors = jnp.array([8.0, 8.0, 4.0], real).reshape(3, 1, 1)
    return 2.0 * velocity, factors * stress


def solution(mesh):
    return jax.shard_map(
        shards,
        mesh=mesh,
        in_specs=(
            P("groups", "curve", ("sub", "pair")),
            P("groups", "curve", ("sub", "pair")),
            P("groups", "curve", ("sub", "pair")),
            P(),
            P(None, ("groups", "curve"), ("sub", "pair")),
            P(("groups", "curve"), ("sub", "pair")),
        ),
        out_specs=(
            P(None, ("groups", "curve"), ("sub", "pair")),
            P(None, ("groups", "curve"), ("sub", "pair")),
        ),
        check_vma=False,
    )
```
